32 devices in a mesh: dp: 8 (over z, x), tensor: 4 (over y, core).
Axes of the slice: x: 2, y: 2, z: 4, core: 2. Of those that a mesh axis runs over, the one named last changes fastest.
Arguments:
- tokens: bfloat16 [16384, 1024], P(('dp', 'tensor')), may hold values from -6 to 6
- cotangent: bfloat16 [16384, 1024], P(('dp', 'tensor')), may hold values from -6 to 6
- lengths: int32 [8, 2], P('dp'), may hold values from 1 to 1024, as said below
- w_heads: float32 [1024, 4096], P('dp', 'tensor'), may hold values from -0.1875 to 0.1875
- first_heads: float32 [1024, 4096], P('dp', 'tensor'), may hold values from -28 to 28
- second_heads: float32 [1024, 4096], P('dp', 'tensor'), may hold values from 81.92 to 327.68
- w_shared: float32 [1024, 288], P('dp'), may hold values from -0.1875 to 0.1875
- first_shared: float32 [1024, 288], P('dp'), may hold values from -80 to 80
- second_shared: float32 [1024, 288], P('dp'), may hold values from 819.2 to 3276.8
- w_out: float32 [1024, 2048], P('dp', 'tensor'), may hold values from -0.125 to 0.125
- first_out: float32 [1024, 2048], P('dp', 'tensor'), may hold values from -64 to 64
- second_out: float32 [1024, 2048], P('dp', 'tensor'), may hold values from 491.52 to 1966.08
- chan_params: float32 [5, 2048], P(None, 'tensor'), may hold values from -2.5 to 2.5
- first_chan: float32 [5, 2048], P(None, 'tensor'), may hold values from -28 to 28
- second_chan: float32 [5, 2048], P(None, 'tensor'), may hold values from 81.92 to 327.68
- bc_params: float32 [5, 256], replicated, may hold values from -2.5 to 2.5
- first_bc: float32 [5, 256], replicated, may hold values from -80 to 80
- second_bc: float32 [5, 256], replicated, may hold values from 819.2 to 3276.8
- head_params: float32 [3, 32], P(None, 'tensor'), may hold values from -7 to 2.8
- first_head: float32 [3, 32], P(None, 'tensor'), may hold values from -224 to 224
- second_head: float32 [3, 32], P(None, 'tensor'), may hold values from 4915.2 to 19660.8
- gains: float32 [3072], replicated, may hold values from 0.48 to 2.16
- first_gains: float32 [3072], replicated, may hold values from -80 to 80
- second_gains: float32 [3072], replicated, may hold values from 819.2 to 3276.8
Outputs:
- output: float32 [16384, 1024], P(('dp', 'tensor'))
- input_grad: float32 [16384, 1024], P(('dp', 'tensor'))
- new_heads: float32 [1024, 4096], P('dp', 'tensor')
- new_first_heads: float32 [1024, 4096], P('dp', 'tensor')
- new_second_heads: float32 [1024, 4096], P('dp', 'tensor')
- new_shared: float32 [1024, 288], P('dp')
- new_first_shared: float32 [1024, 288], P('dp')
- new_second_shared: float32 [1024, 288], P('dp')
- new_out: float32 [1024, 2048], P('dp', 'tensor')
- new_first_out: float32 [1024, 2048], P('dp', 'tensor')
- new_second_out: float32 [1024, 2048], P('dp', 'tensor')
- new_chan: float32 [5, 2048], P(None, 'tensor')
- new_first_chan: float32 [5, 2048], P(None, 'tensor')
- new_second_chan: float32 [5, 2048], P(None, 'tensor')
- new_bc: float32 [5, 256], replicated
- new_first_bc: float32 [5, 256], replicated
- new_second_bc: float32 [5, 256], replicated
- new_head: float32 [3, 32], P(None, 'tensor')
- new_first_head: float32 [3, 32], P(None, 'tensor')
- new_second_head: float32 [3, 32], P(None, 'tensor')
- new_gains: float32 [3072], replicated
- new_first_gains: float32 [3072], replicated
- new_second_gains: float32 [3072], replicated
The draws below stay inside these ranges and needn't reach their ends.
Inputs may be any that keep to these rules, and one draw needn't show every extreme that they name: In every group the lengths sum to at most 2048, and one sequence, in a slot drawn from the seed, has exactly 1024 rows.
All inputs are finite; a program needn't handle non-finite values.
Results may differ from the reference program's by a relative error of at most 0.008.
Values may be sent and summed in bfloat16 or wider, within the bound.
A program may use at most 192 MiB of HBM per device.

```python
import math
import jax
import jax.numpy as jnp
from jax import lax

D = 1024
H = 32
P_SIZE = 64
NS = 128
SPAN = 256
MAXLEN = 1024
STEP = 10
SEQS = 2
DI = 2048
TOK_GRP = 2048
TOKENS = 16384
N_DP = 8


def draw_lengths(key, part):
    key = jax.random.fold_in(key, 11)
    first_key, second_key = jax.random.split(key)
    base_lengths = jax.random.randint(first_key, (N_DP, SEQS), 1, MAXLEN + 1)
    longest = jax.random.randint(second_key, (N_DP, 1), 0, SEQS)
    slots = jnp.arange(SEQS, dtype=jnp.int32)[None, :]
    return jnp.where(slots == longest, MAXLEN, base_lengths).astype(jnp.int32)


def draw_head_params(key, part):
    key = jax.random.fold_in(key, 23)
    rate_key, bias_key, skip_key = jax.random.split(key, 3)
    rates = jnp.exp(jax.random.uniform(rate_key, (H,), jnp.float32, 0.0, 2.8))
    biases = jax.random.uniform(bias_key, (H,), jnp.float32, -6.5, -4.5)
    skips = jax.random.uniform(skip_key, (H,), jnp.float32, 0.5, 1.5)
    return jnp.stack([jnp.log(rates), biases, skips]).astype(jnp.float32)


def draw_gains(key, part):
    key = jax.random.fold_in(key, 37)
    front_key, back_key = jax.random.split(key)
    front = jnp.clip(1.0 + 0.1 * jax.random.normal(front_key, (D,), jnp.float32), 0.6, 1.4)
    ramp = 0.6 + 1.2 * jnp.arange(H * P_SIZE, dtype=jnp.float32) / (H * P_SIZE)
    back = ramp * jax.random.uniform(back_key, (H * P_SIZE,), jnp.float32, 0.8, 1.2)
    return jnp.concatenate([front, back]).astype(jnp.float32)


def shard_levels(rng, dims, cuts, least, top_value):
    level, own = 1.0, jax.random.fold_in(rng, 6)
    for dim, parts in cuts:
        draws = jnp.exp(jax.random.uniform(jax.random.fold_in(own, dim), (parts,), jnp.float32, least / len(cuts), top_value / len(cuts)))
        level = level * jnp.repeat(draws, dims[dim] // parts).reshape([-1 if axis == dim else 1 for axis in range(len(dims))])
    return level


def centred(stream_key, extent, scale, bound, pieces=(), kind=jnp.bfloat16):
    factor_of = shard_levels(stream_key, extent, pieces, -0.22, 0.18) if pieces else 1.0
    values = jax.random.normal(stream_key, extent, jnp.float32) * scale * factor_of
    return jnp.minimum(jnp.maximum(values, -bound), bound).astype(kind)


def setup_inputs(seed: int = 0) -> dict:
    seeds = jax.random.split(jax.random.key(seed), 25)
    tokens = centred(seeds[0], (TOKENS, D), 1.0, 6.0, ((0, 32),))
    cotangent = centred(seeds[1], (TOKENS, D), 1.0, 6.0, ((0, 32),))
    lengths = draw_lengths(jax.random.fold_in(seeds[24], 71), 0)
    w_heads = centred(seeds[3], (D, 2 * DI), D ** -0.5, 0.1875, ((0, 8), (1, 4)), jnp.float32)
    first_heads = centred(seeds[4], (D, 2 * DI), (0.035 * TOKENS ** 0.5), 28.0, ((0, 8), (1, 4)), jnp.float32)
    second_heads = jnp.clip(jnp.exp(math.log(327.68) - 1.3862944 * jax.random.uniform(seeds[5], (D, 2 * DI), jnp.float32) ** shard_levels(seeds[5], (D, 2 * DI), ((0, 8), (1, 4)), -0.2, 0.2)), 81.92, 327.68)
    w_shared = centred(seeds[6], (D, 2 * NS + H), D ** -0.5, 0.1875, ((0, 8),), jnp.float32)
    first_shared = centred(seeds[7], (D, 2 * NS + H), (0.1 * TOKENS ** 0.5), 80.0, ((0, 8),), jnp.float32)
    second_shared = jnp.clip(jnp.exp(math.log(3276.8) - 1.3862944 * jax.random.uniform(seeds[8], (D, 2 * NS + H), jnp.float32) ** shard_levels(seeds[8], (D, 2 * NS + H), ((0, 8),), -0.2, 0.2)), 819.2, 3276.8)
    w_out = centred(seeds[9], (D, DI), DI ** -0.5, 0.125, ((0, 8), (1, 4)), jnp.float32)
    first_out = centred(seeds[10], (D, DI), (0.08 * TOKENS ** 0.5), 64.0, ((0, 8), (1, 4)), jnp.float32)
    second_out = jnp.clip(jnp.exp(math.log(1966.08) - 1.3862944 * jax.random.uniform(seeds[11], (D, DI), jnp.float32) ** shard_levels(seeds[11], (D, DI), ((0, 8), (1, 4)), -0.2, 0.2)), 491.52, 1966.08)
    chan_params = centred(seeds[12], (5, DI), 0.5, 2.5, ((1, 4),), jnp.float32)
    first_chan = centred(seeds[13], (5, DI), (0.035 * TOKENS ** 0.5), 28.0, ((1, 4),), jnp.float32)
    second_chan = jnp.clip(jnp.exp(math.log(327.68) - 1.3862944 * jax.random.uniform(seeds[14], (5, DI), jnp.float32) ** shard_levels(seeds[14], (5, DI), ((1, 4),), -0.2, 0.2)), 81.92, 327.68)
    bc_params = centred(seeds[15], (5, 2 * NS), 0.5, 2.5, (), jnp.float32)
    first_bc = centred(seeds[16], (5, 2 * NS), (0.1 * TOKENS ** 0.5), 80.0, (), jnp.float32)
    second_bc = jnp.clip(jnp.exp(jax.random.uniform(seeds[17], (5, 2 * NS), jnp.float32, math.log(819.2), math.log(3276.8))), 819.2, 3276.8)
    head_params = draw_head_params(jax.random.fold_in(seeds[24], 71), 0)
    first_head = centred(seeds[19], (3, H), (0.3 * TOKENS ** 0.5), 224.0, ((1, 4),), jnp.float32)
    second_head = jnp.clip(jnp.exp(math.log(19660.8) - 1.3862944 * jax.random.uniform(seeds[20], (3, H), jnp.float32) ** shard_levels(seeds[20], (3, H), ((1, 4),), -0.2, 0.2)), 4915.2, 19660.8)
    gains = draw_gains(jax.random.fold_in(seeds[24], 71), 0)
    first_gains = centred(seeds[22], (D + DI,), (0.1 * TOKENS ** 0.5), 80.0, (), jnp.float32)
    second_gains = jnp.clip(jnp.exp(jax.random.uniform(seeds[23], (D + DI,), jnp.float32, math.log(819.2), math.log(3276.8))), 819.2, 3276.8)
    return dict(tokens=tokens, cotangent=cotangent, lengths=lengths, w_heads=w_heads, first_heads=first_heads, second_heads=second_heads, w_shared=w_shared, first_shared=first_shared, second_shared=second_shared, w_out=w_out, first_out=first_out, second_out=second_out, chan_params=chan_params, first_chan=first_chan, second_chan=second_chan, bc_params=bc_params, first_bc=first_bc, second_bc=second_bc, head_params=head_params, first_head=first_head, second_head=second_head, gains=gains, first_gains=first_gains, second_gains=second_gains)


NORM_EPS = 1e-05
BETA_ONE = 0.9
BETA_TWO = 0.95
ADAM_EPS = 1e-08
MATRIX_RATE = 0.03
SMALL_RATE = 0.1
HEAD_RATE = 1.0
GAIN_RATE = 0.5
WEIGHT_DECAY = 0.1
HIGHEST_PREC = lax.Precision.HIGHEST

@jax.custom_vjp
def low(v):
    return lax.optimization_barrier(v.astype(jnp.bfloat16)).astype(jnp.float32)

@jax.custom_vjp
def low_back(v):
    return v

def low_keep(v):
    return (low(v), None)

def low_pass(kept, grad):
    return (grad,)

def back_keep(v):
    return (v, None)

def back_low(kept, grad):
    return (low(grad),)
low.defvjp(low_keep, low_pass)
low_back.defvjp(back_keep, back_low)

def segment_ids(seq_lengths, group_rows):
    seq_ends = jnp.cumsum(seq_lengths).astype(jnp.int32)
    positions = jnp.arange(group_rows, dtype=jnp.int32)
    return lax.optimization_barrier(jnp.sum((positions[:, None] >= seq_ends[None, :]).astype(jnp.int32), axis=1)).astype(jnp.int32)

def causal_conv(raw_vals, conv_taps, seq_ids):
    result = conv_taps[4][None, :] + conv_taps[3][None, :] * raw_vals
    for offset in range(1, 4):
        shifted = jnp.concatenate([jnp.zeros((offset, raw_vals.shape[1]), raw_vals.dtype), raw_vals[:-offset]], axis=0)
        shifted_ids = jnp.concatenate([jnp.full((offset,), -1, jnp.int32), seq_ids[:-offset]])
        same_seq = (shifted_ids == seq_ids).astype(raw_vals.dtype)
        result = result + conv_taps[3 - offset][None, :] * shifted * same_seq[:, None]
    return result

def state_space(values, in_maps, out_maps, log_decay, step_size, seq_ids, skip_gain):
    seq_rows, head_count, head_size = values.shape
    state_size = in_maps.shape[1]
    blocks = seq_rows // SPAN
    values_c = values.reshape(blocks, SPAN, head_count, head_size)
    in_c = in_maps.reshape(blocks, SPAN, state_size)
    out_c = out_maps.reshape(blocks, SPAN, state_size)
    decay_c = jnp.transpose(jnp.cumsum(log_decay.reshape(blocks, SPAN, head_count), axis=1), (0, 2, 1))
    step_c = jnp.transpose(step_size.reshape(blocks, SPAN, head_count), (0, 2, 1))
    ids_c = seq_ids.reshape(blocks, SPAN)
    last_ids = ids_c[:, -1]
    prior_ids = jnp.concatenate([jnp.full((1,), -1, jnp.int32), last_ids[:-1]])
    positions = jnp.arange(SPAN, dtype=jnp.int32)
    allowed = (ids_c[:, :, None] == ids_c[:, None, :]) & (positions[:, None] >= positions[None, :])[None]
    allowed = allowed[:, None, :, :]
    spread = decay_c[:, :, :, None] - decay_c[:, :, None, :]
    kernel = jnp.where(allowed, jnp.exp(jnp.where(allowed, spread, 0.0)), 0.0)
    inner_prod = jnp.einsum('cqn,ckn->cqk', out_c, in_c, precision=HIGHEST_PREC)
    mixing = kernel * inner_prod[:, None, :, :] * step_c[:, :, None, :]
    local_part = jnp.einsum('chqk,ckhp->cqhp', mixing, values_c, precision=HIGHEST_PREC)
    tail_decay = decay_c[:, :, -1]
    same_last = (ids_c == last_ids[:, None]).astype(jnp.float32)
    carry_w = jnp.exp(tail_decay[:, :, None] - decay_c) * step_c * same_last[:, None, :]
    fresh_states = jnp.einsum('chk,ckn,ckhp->chpn', carry_w, in_c, values_c, precision=HIGHEST_PREC)
    through = (last_ids == prior_ids).astype(jnp.float32)[:, None] * jnp.exp(tail_decay)

    def advance(carry_state, block_item):
        fresh_block, factor = block_item
        return (factor[:, None, None] * carry_state + fresh_block, carry_state)
    start_state = jnp.zeros((head_count, head_size, state_size), jnp.float32)
    _, entering = lax.scan(advance, start_state, (fresh_states, through))
    reach_w = jnp.exp(decay_c) * (ids_c == prior_ids[:, None]).astype(jnp.float32)[:, None, :]
    carried = jnp.einsum('cqn,chpn->cqhp', out_c, entering, precision=HIGHEST_PREC)
    carried = carried * jnp.transpose(reach_w, (0, 2, 1))[:, :, :, None]
    result = (local_part + carried).reshape(seq_rows, head_count, head_size)
    return result + skip_gain[None, :, None] * values

def block_forward(tokens, w_heads, w_shared, w_out, chan_params, bc_params, head_params, gains, lengths):
    heads_low = low(w_heads)
    shared_low = low(w_shared)
    out_low = low(w_out)
    norm_gain = gains[:D]
    gate_gain = gains[D:]

    def one_group(group_in, group_lengths):
        seq_ids = segment_ids(group_lengths, TOK_GRP)
        valid_rows = (seq_ids < SEQS).astype(jnp.float32)
        norm_scale = lax.rsqrt(lax.optimization_barrier(jnp.mean(group_in * group_in, axis=1, keepdims=True)) + NORM_EPS)
        normed = low(group_in * norm_scale * norm_gain[None, :])
        head_cols = low_back(jnp.dot(normed, heads_low, precision=HIGHEST_PREC)).reshape(TOK_GRP, H, 2, P_SIZE)
        shared = low_back(jnp.dot(normed, shared_low, precision=HIGHEST_PREC))
        gate_vals = head_cols[:, :, 0, :]
        value_raw = head_cols[:, :, 1, :].reshape(TOK_GRP, H * P_SIZE)
        conv_value = low(jax.nn.silu(causal_conv(value_raw, chan_params, seq_ids)))
        conv_bc = low(jax.nn.silu(causal_conv(shared[:, :2 * NS], bc_params, seq_ids)))
        step_size = jax.nn.softplus(shared[:, 2 * NS:] + head_params[1][None, :])
        log_decay = -jnp.exp(head_params[0])[None, :] * step_size
        ssd_out = state_space(conv_value.reshape(TOK_GRP, H, P_SIZE), conv_bc[:, :NS], conv_bc[:, NS:], log_decay, step_size, seq_ids, head_params[2])
        gated_vals = (ssd_out * jax.nn.silu(gate_vals)).reshape(TOK_GRP, H * P_SIZE)
        inv_gate = lax.rsqrt(lax.optimization_barrier(jnp.mean(gated_vals * gated_vals, axis=1, keepdims=True)) + NORM_EPS)
        normal_out = low(gated_vals * inv_gate * gate_gain[None, :])
        branch = jnp.dot(normal_out, out_low.T, precision=HIGHEST_PREC)
        return group_in + valid_rows[:, None] * branch
    groups = tokens.reshape(N_DP, TOK_GRP, D)
    results = lax.map(lambda group_item: jax.checkpoint(one_group)(group_item[0], group_item[1]), (groups, lengths))
    return results.reshape(TOKENS, D)

def adam_step(weight, grad, first_moment, second_moment, rate, decay_rate):
    first_new = BETA_ONE * first_moment + (1.0 - BETA_ONE) * grad
    second_new = BETA_TWO * second_moment + (1.0 - BETA_TWO) * grad * grad
    first_fix = 1.0 - BETA_ONE ** STEP
    second_fix = 1.0 - BETA_TWO ** STEP
    update = first_new / first_fix / (jnp.sqrt(second_new / second_fix) + ADAM_EPS)
    return (weight - rate * (update + decay_rate * weight), first_new, second_new)

def reference(tokens, cotangent, lengths, w_heads, first_heads, second_heads, w_shared, first_shared, second_shared, w_out, first_out, second_out, chan_params, first_chan, second_chan, bc_params, first_bc, second_bc, head_params, first_head, second_head, gains, first_gains, second_gains):

    def forward(tokens_f, heads_f, shared_f, out_f, chan_f, bc_f, head_f, gains_f):
        return block_forward(tokens_f, heads_f, shared_f, out_f, chan_f, bc_f, head_f, gains_f, lengths)
    output, pullback = jax.vjp(forward, tokens.astype(jnp.float32), w_heads, w_shared, w_out, chan_params, bc_params, head_params, gains)
    gradients = pullback(cotangent.astype(jnp.float32))
    input_grad = gradients[0]
    new_heads, new_first_heads, new_second_heads = adam_step(w_heads, gradients[1], first_heads, second_heads, MATRIX_RATE, WEIGHT_DECAY)
    new_shared, new_first_shared, new_second_shared = adam_step(w_shared, gradients[2], first_shared, second_shared, MATRIX_RATE, WEIGHT_DECAY)
    new_out, new_first_out, new_second_out = adam_step(w_out, gradients[3], first_out, second_out, MATRIX_RATE, WEIGHT_DECAY)
    new_chan, new_first_chan, new_second_chan = adam_step(chan_params, gradients[4], first_chan, second_chan, SMALL_RATE, 0.0)
    new_bc, new_first_bc, new_second_bc = adam_step(bc_params, gradients[5], first_bc, second_bc, SMALL_RATE, 0.0)
    new_head, new_first_head, new_second_head = adam_step(head_params, gradients[6], first_head, second_head, HEAD_RATE, 0.0)
    new_gains, new_first_gains, new_second_gains = adam_step(gains, gradients[7], first_gains, second_gains, GAIN_RATE, 0.0)
    return (output, input_grad, new_heads, new_first_heads, new_second_heads, new_shared, new_first_shared, new_second_shared, new_out, new_first_out, new_second_out, new_chan, new_first_chan, new_second_chan, new_bc, new_first_bc, new_second_bc, new_head, new_first_head, new_second_head, new_gains, new_first_gains, new_second_gains)
```

```python
import jax
import jax.numpy as jnp
from jax import lax
from jax.sharding import PartitionSpec as P

SPAN = 256
STEP = 10


NORM_EPS = 1e-05
BETA_ONE = 0.9
BETA_TWO = 0.95
ADAM_EPS = 1e-08
MATRIX_RATE = 0.03
SMALL_RATE = 0.1
HEAD_RATE = 1.0
GAIN_RATE = 0.5
WEIGHT_DECAY = 0.1
HIGHEST_PREC = lax.Precision.HIGHEST


def segment_ids(seq_lengths, group_rows):
    seq_ends = jnp.cumsum(seq_lengths)
    positions = jnp.arange(group_rows, dtype=jnp.int32)
    return jnp.sum((positions[:, None] >= seq_ends[None, :]).astype(jnp.int32), axis=1)


def causal_conv(raw_vals, conv_taps, seq_ids):
    result = conv_taps[4][None, :] + conv_taps[3][None, :] * raw_vals
    for offset in range(1, 4):
        shifted = jnp.concatenate(
            [jnp.zeros((offset, raw_vals.shape[1]), raw_vals.dtype), raw_vals[:-offset]], axis=0
        )
        shifted_ids = jnp.concatenate([jnp.full((offset,), -1, jnp.int32), seq_ids[:-offset]])
        same_seq = (shifted_ids == seq_ids).astype(raw_vals.dtype)
        result = result + conv_taps[3 - offset][None, :] * shifted * same_seq[:, None]
    return result


def state_space(values, in_maps, out_maps, log_decay, step_size, seq_ids, skip_gain):
    seq_rows, head_count, head_size = values.shape
    state_size = in_maps.shape[1]
    blocks = seq_rows // SPAN
    values_c = values.reshape(blocks, SPAN, head_count, head_size)
    in_c = in_maps.reshape(blocks, SPAN, state_size)
    out_c = out_maps.reshape(blocks, SPAN, state_size)
    decay_c = jnp.transpose(
        jnp.cumsum(log_decay.reshape(blocks, SPAN, head_count), axis=1), (0, 2, 1)
    )
    step_c = jnp.transpose(step_size.reshape(blocks, SPAN, head_count), (0, 2, 1))
    ids_c = seq_ids.reshape(blocks, SPAN)
    last_ids = ids_c[:, -1]
    prior_ids = jnp.concatenate([jnp.full((1,), -1, jnp.int32), last_ids[:-1]])
    positions = jnp.arange(SPAN, dtype=jnp.int32)
    allowed = (ids_c[:, :, None] == ids_c[:, None, :]) & (positions[:, None] >= positions[None, :])[
        None
    ]
    allowed = allowed[:, None, :, :]
    spread = decay_c[:, :, :, None] - decay_c[:, :, None, :]
    kernel = jnp.where(allowed, jnp.exp(jnp.where(allowed, spread, 0.0)), 0.0)
    inner_prod = jnp.einsum("cqn,ckn->cqk", out_c, in_c, precision=HIGHEST_PREC)
    mixing = kernel * inner_prod[:, None, :, :] * step_c[:, :, None, :]
    local_part = jnp.einsum("chqk,ckhp->cqhp", mixing, values_c, precision=HIGHEST_PREC)
    tail_decay = decay_c[:, :, -1]
    same_last = (ids_c == last_ids[:, None]).astype(jnp.float32)
    carry_w = jnp.exp(tail_decay[:, :, None] - decay_c) * step_c * same_last[:, None, :]
    fresh_states = jnp.einsum("chk,ckn,ckhp->chpn", carry_w, in_c, values_c, precision=HIGHEST_PREC)
    through = (last_ids == prior_ids).astype(jnp.float32)[:, None] * jnp.exp(tail_decay)

    def advance(carry_state, block_item):
        fresh_block, factor = block_item
        return (factor[:, None, None] * carry_state + fresh_block, carry_state)

    start_state = jnp.zeros((head_count, head_size, state_size), jnp.float32)
    _, entering = lax.scan(advance, start_state, (fresh_states, through))
    reach_w = jnp.exp(decay_c) * (ids_c == prior_ids[:, None]).astype(jnp.float32)[:, None, :]
    carried = jnp.einsum("cqn,chpn->cqhp", out_c, entering, precision=HIGHEST_PREC)
    carried = carried * jnp.transpose(reach_w, (0, 2, 1))[:, :, :, None]
    result = (local_part + carried).reshape(seq_rows, head_count, head_size)
    return result + skip_gain[None, :, None] * values


def contract_last(left, right):
    return lax.dot_general(
        left, right, (((1,), (1,)), ((), ())), preferred_element_type=jnp.float32
    )


def contract_first(left, right):
    return lax.dot_general(
        left, right, (((0,), (0,)), ((), ())), preferred_element_type=jnp.float32
    )


def adam_step(weight, grad, first_moment, second_moment, rate, decay_rate):
    first_new = BETA_ONE * first_moment + (1.0 - BETA_ONE) * grad
    second_new = BETA_TWO * second_moment + (1.0 - BETA_TWO) * grad * grad
    first_fix = 1.0 - BETA_ONE**STEP
    second_fix = 1.0 - BETA_TWO**STEP
    update = first_new / first_fix / (jnp.sqrt(second_new / second_fix) + ADAM_EPS)
    return (weight - rate * (update + decay_rate * weight), first_new, second_new)


def swap(vals, axis, bit):
    ways = lax.axis_size(axis)
    return lax.ppermute(vals, axis, [(i, i ^ bit) for i in range(ways)])


def axis_bits(axis):
    return [1 << i for i in range(lax.axis_size(axis).bit_length() - 1)]


def gather_rows(vals, axis, order):
    rows = vals.shape[0]
    ways = lax.axis_size(axis)
    pos = lax.axis_index(axis)
    bits = axis_bits(axis)
    held = vals.reshape((1,) * len(bits) + vals.shape)
    for bit in order:
        dim = len(bits) - bit.bit_length()
        other = swap(held, axis, bit)
        upper = (pos & bit) != 0
        held = jnp.concatenate(
            [jnp.where(upper, other, held), jnp.where(upper, held, other)], axis=dim
        )
    return held.reshape((ways * rows,) + vals.shape[1:])


def scatter_rows(vals, axis, order):
    ways = lax.axis_size(axis)
    pos = lax.axis_index(axis)
    bits = axis_bits(axis)
    rows = vals.shape[0] // ways
    held = vals.reshape((2,) * len(bits) + (rows,) + vals.shape[1:])
    for bit in order:
        dim = len(bits) - bit.bit_length()
        mine = (pos & bit) // bit
        keep = lax.dynamic_slice_in_dim(held, mine, 1, dim)
        send = lax.dynamic_slice_in_dim(held, 1 - mine, 1, dim).astype(jnp.bfloat16)
        held = keep.astype(jnp.float32) + swap(send, axis, bit).astype(jnp.float32)
    return held.reshape((rows,) + vals.shape[1:])


def sum_all(vals, axis):
    for bit in axis_bits(axis):
        vals = vals + swap(vals, axis, bit)
    return vals


def gather_two(vals, axis):
    bits = axis_bits(axis)
    half = (vals.shape[1] // 256) * 128
    return jnp.concatenate(
        [
            gather_rows(vals[:, :half], axis, bits[::-1]),
            gather_rows(vals[:, half:], axis, bits[:1] + bits[:0:-1]),
        ],
        axis=1,
    )


def scatter_two(vals, axis):
    bits = axis_bits(axis)
    half = (vals.shape[1] // 256) * 128
    return jnp.concatenate(
        [
            scatter_rows(vals[:, :half], axis, bits),
            scatter_rows(vals[:, half:], axis, bits[1:] + bits[:1]),
        ],
        axis=1,
    )


def shards(
    tokens,
    cotangent,
    lengths,
    w_heads,
    first_heads,
    second_heads,
    w_shared,
    first_shared,
    second_shared,
    w_out,
    first_out,
    second_out,
    chan_params,
    first_chan,
    second_chan,
    bc_params,
    first_bc,
    second_bc,
    head_params,
    first_head,
    second_head,
    gains,
    first_gains,
    second_gains,
):
    tensor_ways = lax.axis_size("tensor")
    tensor_pos = lax.axis_index("tensor")
    own_rows = tokens.shape[0]
    group_rows = own_rows * tensor_ways
    model_width = tokens.shape[1]
    own_heads = head_params.shape[1]
    all_heads = own_heads * tensor_ways
    own_inner = chan_params.shape[1]
    all_inner = own_inner * tensor_ways
    head_size = own_inner // own_heads
    state_size = bc_params.shape[1] // 2
    seq_ids = segment_ids(lengths[0], group_rows)
    valid_rows = (seq_ids < lengths.shape[1]).astype(jnp.float32)
    own_valid = lax.dynamic_slice_in_dim(valid_rows, tensor_pos * own_rows, own_rows, 0)[:, None]
    norm_gain = gains[:model_width]
    gate_gain = gains[model_width:]
    inputs_f = tokens.astype(jnp.float32)
    norm_scale = lax.rsqrt(jnp.mean(inputs_f * inputs_f, axis=1, keepdims=True) + NORM_EPS)
    normed = (inputs_f * norm_scale * norm_gain[None, :]).astype(jnp.bfloat16)
    gathered = gather_rows(normed, "tensor", (2, 1))
    in_width = w_heads.shape[1]
    in_full = gather_two(
        jnp.concatenate([w_heads.astype(jnp.bfloat16), w_shared.astype(jnp.bfloat16)], axis=1), "dp"
    )
    heads_full, shared_full = in_full[:, :in_width], in_full[:, in_width:]
    out_cols = gather_two(w_out.astype(jnp.bfloat16), "dp")
    head_cols = jnp.dot(gathered, heads_full, preferred_element_type=jnp.float32).reshape(
        group_rows, own_heads, 2, head_size
    )
    shared = jnp.dot(gathered, shared_full, preferred_element_type=jnp.float32)
    gate_vals = head_cols[:, :, 0, :]
    conv_in = jnp.concatenate(
        [head_cols[:, :, 1, :].reshape(group_rows, own_inner), shared[:, : 2 * state_size]], axis=1
    )
    conv_taps = jnp.concatenate([chan_params, bc_params], axis=1)

    def convolve(raw_vals, taps_all):
        return jax.nn.silu(causal_conv(raw_vals, taps_all, seq_ids))

    conv_out, conv_pull = jax.vjp(convolve, conv_in, conv_taps)
    conv_low = lax.optimization_barrier(conv_out.astype(jnp.bfloat16)).astype(jnp.float32)
    step_raw = lax.dynamic_slice_in_dim(
        shared[:, 2 * state_size :], tensor_pos * own_heads, own_heads, 1
    )

    def mixer(conv_vals, gate_in, step_in, head_vals):
        step_size = jax.nn.softplus(step_in + head_vals[1][None, :])
        log_decay = -jnp.exp(head_vals[0])[None, :] * step_size
        value_part = conv_vals[:, :own_inner].reshape(group_rows, own_heads, head_size)
        in_maps = conv_vals[:, own_inner : own_inner + state_size]
        out_maps = conv_vals[:, own_inner + state_size :]
        ssd_out = state_space(
            value_part, in_maps, out_maps, log_decay, step_size, seq_ids, head_vals[2]
        )
        return (ssd_out * jax.nn.silu(gate_in)).reshape(group_rows, own_inner)

    gated_vals, mixer_pull = jax.vjp(mixer, conv_low, gate_vals, step_raw, head_params)
    cotangent_f = cotangent.astype(jnp.float32)
    masked = (cotangent_f * own_valid).astype(jnp.bfloat16)
    own_gain = lax.dynamic_slice_in_dim(gate_gain, tensor_pos * own_inner, own_inner, 0)[None, :]
    square_sum = lax.psum(jnp.sum(gated_vals * gated_vals, axis=1), "tensor")
    inv_gate = lax.rsqrt(square_sum / all_inner + NORM_EPS)[:, None]
    normal_out = (gated_vals * inv_gate * own_gain).astype(jnp.bfloat16)
    branch = scatter_rows(contract_last(normal_out, out_cols), "tensor", (1, 2))
    masked_all = gather_rows(masked, "tensor", (2, 1))
    d_normal = jnp.dot(masked_all, out_cols, preferred_element_type=jnp.float32)
    weighted = d_normal * own_gain
    row_dot = lax.psum(jnp.sum(gated_vals * weighted, axis=1), "tensor")[:, None]
    d_gated = inv_gate * weighted - gated_vals * inv_gate**3 * row_dot / all_inner
    own_gain_grad = jnp.sum(gated_vals * inv_gate * d_normal, axis=0)
    gate_gain_grad = lax.dynamic_update_slice_in_dim(
        jnp.zeros((all_inner,), jnp.float32), own_gain_grad, tensor_pos * own_inner, 0
    )
    out_grad = contract_first(masked_all, normal_out)
    output = inputs_f + own_valid * branch
    d_conv, d_gate, d_step, d_head = mixer_pull(d_gated)
    d_raw, d_taps = conv_pull(d_conv)
    d_value = d_raw[:, :own_inner].reshape(group_rows, own_heads, head_size)
    d_cols = (
        jnp.stack([d_gate, d_value], axis=2).reshape(group_rows, 2 * own_inner).astype(jnp.bfloat16)
    )
    d_step_all = lax.dynamic_update_slice_in_dim(
        jnp.zeros((group_rows, all_heads), jnp.float32), d_step, tensor_pos * own_heads, 1
    )
    d_shared_part = jnp.concatenate([d_raw[:, own_inner:], d_step_all], axis=1)
    d_normed_part = contract_last(d_cols, heads_full)
    d_normed_rows, d_shared_rows = (
        scatter_rows(d_normed_part, "tensor", (1, 2)),
        scatter_rows(d_shared_part, "tensor", (1, 2)),
    )
    d_shared_low = d_shared_rows.astype(jnp.bfloat16)
    d_normed = d_normed_rows + contract_last(d_shared_low, shared_full)
    weighted_in = d_normed * norm_gain[None, :]
    in_dot = jnp.sum(inputs_f * weighted_in, axis=1, keepdims=True)
    input_grad = (
        cotangent_f + norm_scale * weighted_in - inputs_f * norm_scale**3 * in_dot / model_width
    )
    heads_grad = contract_first(gathered, d_cols)
    heads_shard, out_shard = (
        scatter_two(heads_grad, "dp"),
        scatter_two(out_grad, "dp"),
    )
    norm_gain_grad = jnp.sum(inputs_f * norm_scale * d_normed, axis=0)
    own_sums = sum_all(
        jnp.concatenate(
            [
                norm_gain_grad,
                d_taps[:, own_inner:].reshape(-1),
                gate_gain_grad,
                d_taps[:, :own_inner].reshape(-1),
                d_head.reshape(-1),
            ]
        ),
        "dp",
    )
    shared_part = scatter_rows(
        contract_first(normed, d_shared_low), "dp", axis_bits("dp")
    )
    shared_rows, shared_width = shared_part.shape
    gain_ends = model_width + 10 * state_size
    chan_begin = gain_ends + all_inner
    head_begin = chan_begin + 5 * own_inner
    ring_sums = sum_all(
        jnp.concatenate([own_sums[:chan_begin], shared_part.reshape(-1)]), "tensor"
    )
    gain_sum = jnp.concatenate([ring_sums[:model_width], ring_sums[gain_ends:chan_begin]])
    bc_sum = ring_sums[model_width:gain_ends].reshape(5, 2 * state_size)
    shared_shard = ring_sums[chan_begin:].reshape(shared_rows, shared_width)
    chan_grad = own_sums[chan_begin:head_begin].reshape(5, own_inner)
    head_grad = own_sums[head_begin:].reshape(3, own_heads)
    new_heads, new_first_heads, new_second_heads = adam_step(
        w_heads, heads_shard, first_heads, second_heads, MATRIX_RATE, WEIGHT_DECAY
    )
    new_shared, new_first_shared, new_second_shared = adam_step(
        w_shared, shared_shard, first_shared, second_shared, MATRIX_RATE, WEIGHT_DECAY
    )
    new_out, new_first_out, new_second_out = adam_step(
        w_out, out_shard, first_out, second_out, MATRIX_RATE, WEIGHT_DECAY
    )
    new_chan, new_first_chan, new_second_chan = adam_step(
        chan_params, chan_grad, first_chan, second_chan, SMALL_RATE, 0.0
    )
    new_bc, new_first_bc, new_second_bc = adam_step(
        bc_params, bc_sum, first_bc, second_bc, SMALL_RATE, 0.0
    )
    new_head, new_first_head, new_second_head = adam_step(
        head_params, head_grad, first_head, second_head, HEAD_RATE, 0.0
    )
    new_gains, new_first_gains, new_second_gains = adam_step(
        gains, gain_sum, first_gains, second_gains, GAIN_RATE, 0.0
    )
    return (
        output,
        input_grad,
        new_heads,
        new_first_heads,
        new_second_heads,
        new_shared,
        new_first_shared,
        new_second_shared,
        new_out,
        new_first_out,
        new_second_out,
        new_chan,
        new_first_chan,
        new_second_chan,
        new_bc,
        new_first_bc,
        new_second_bc,
        new_head,
        new_first_head,
        new_second_head,
        new_gains,
        new_first_gains,
        new_second_gains,
    )


def solution(mesh):
    return jax.shard_map(
        shards,
        mesh=mesh,
        in_specs=(
            P(("dp", "tensor"), None),
            P(("dp", "tensor"), None),
            P("dp", None),
            P("dp", "tensor"),
            P("dp", "tensor"),
            P("dp", "tensor"),
            P("dp", None),
            P("dp", None),
            P("dp", None),
            P("dp", "tensor"),
            P("dp", "tensor"),
            P("dp", "tensor"),
            P(None, "tensor"),
            P(None, "tensor"),
            P(None, "tensor"),
            P(),
            P(),
            P(),
            P(None, "tensor"),
            P(None, "tensor"),
            P(None, "tensor"),
            P(),
            P(),
            P(),
        ),
        out_specs=(
            P(("dp", "tensor"), None),
            P(("dp", "tensor"), None),
            P("dp", "tensor"),
            P("dp", "tensor"),
            P("dp", "tensor"),
            P("dp", None),
            P("dp", None),
            P("dp", None),
            P("dp", "tensor"),
            P("dp", "tensor"),
            P("dp", "tensor"),
            P(None, "tensor"),
            P(None, "tensor"),
            P(None, "tensor"),
            P(),
            P(),
            P(),
            P(None, "tensor"),
            P(None, "tensor"),
            P(None, "tensor"),
            P(),
            P(),
            P(),
        ),
        check_vma=False,
    )
```

```python
import jax
import jax.numpy as jnp
from jax import lax
from jax.experimental import pallas as pl
from jax.experimental.pallas import tpu as pltpu
from jax.sharding import PartitionSpec as P

SPAN = 256
STEP = 10


NORM_EPS = 1e-05
BETA_ONE = 0.9
BETA_TWO = 0.95
ADAM_EPS = 1e-08
MATRIX_RATE = 0.03
SMALL_RATE = 0.1
HEAD_RATE = 1.0
GAIN_RATE = 0.5
WEIGHT_DECAY = 0.1
HIGHEST_PREC = lax.Precision.HIGHEST


def segment_ids(seq_lengths, group_rows):
    seq_ends = jnp.cumsum(seq_lengths)
    positions = jnp.arange(group_rows, dtype=jnp.int32)
    return jnp.sum((positions[:, None] >= seq_ends[None, :]).astype(jnp.int32), axis=1)


LANES = 128
KERNEL_VMEM = 56 * 1024 * 1024


def silu_slope(vals, sig):
    return sig * (1.0 + vals * (1.0 - sig))


def split_halves(vals):
    high = vals.astype(jnp.bfloat16)
    rest = (vals - high.astype(jnp.float32)).astype(jnp.bfloat16)
    return jnp.concatenate([high, rest], axis=1)


def mm(left, right):
    return jnp.dot(left, right, preferred_element_type=jnp.float32)


def ids_at(positions, ends_ref):
    ids = jnp.zeros_like(positions)
    for slot in range(ends_ref.shape[0]):
        ids = ids + jnp.where(positions >= ends_ref[slot], 1, 0)
    return ids


def block_setup(block, ends_ref, step_raw, head_ref, spread_ref):
    begin = block * SPAN
    col = lax.broadcasted_iota(jnp.int32, (SPAN, 1), 0)
    row = lax.broadcasted_iota(jnp.int32, (1, SPAN), 1)
    id_col = ids_at(col + begin, ends_ref)
    id_row = ids_at(row + begin, ends_ref)
    prior, last = jnp.int32(0), jnp.int32(0)
    for slot in range(ends_ref.shape[0]):
        prior = prior + jnp.where(begin - 1 >= ends_ref[slot], 1, 0)
        last = last + jnp.where(begin + SPAN - 1 >= ends_ref[slot], 1, 0)
    prior = jnp.where(block == 0, -1, prior)
    pre_step = step_raw + head_ref[1:2, :]
    step = jnp.maximum(pre_step, 0.0) + jnp.log1p(jnp.exp(-jnp.abs(pre_step)))
    decay = -jnp.exp(head_ref[0:1, :]) * step
    lower = jnp.where(col >= row, 1.0, 0.0)
    total = jnp.dot(
        lower, decay, precision=HIGHEST_PREC, preferred_element_type=jnp.float32
    )
    tail = total[SPAN - 1 : SPAN, :]
    reach = jnp.exp(total) * jnp.where(id_col == prior, 1.0, 0.0)
    leave = jnp.exp(tail - total) * jnp.where(id_col == last, 1.0, 0.0)
    through = jnp.exp(tail) * jnp.where(last == prior, 1.0, 0.0)
    stacked = jnp.concatenate([step, reach, leave, jnp.broadcast_to(through, (8, LANES))], axis=0)
    spread = mm(split_halves(stacked), spread_ref[...])
    return (
        col,
        row,
        id_col,
        id_row,
        pre_step,
        decay,
        total,
        spread[:SPAN],
        spread[SPAN : 2 * SPAN],
        spread[2 * SPAN : 3 * SPAN],
        spread[3 * SPAN : 3 * SPAN + 1],
    )


def forward_kernel(
    ends_ref,
    rows_ref,
    weight_ref,
    taps_ref,
    head_ref,
    skip_ref,
    spread_ref,
    gate_ref,
    raw_ref,
    pre_ref,
    conv_ref,
    step_ref,
    ssd_ref,
    gated_ref,
    state_ref,
    ext_ref,
    carry_ref,
):
    block = pl.program_id(0)
    inner = gate_ref.shape[1]
    width = raw_ref.shape[1]
    states = (width - inner) // 2

    @pl.when(block == 0)
    def _():
        carry_ref[...] = jnp.zeros_like(carry_ref)
        ext_ref[...] = jnp.zeros_like(ext_ref)

    cols = mm(rows_ref[...], weight_ref[...])
    gate = cols[:, :inner]
    raw = cols[:, inner : inner + width]
    step_raw = cols[:, inner + width :]
    gate_ref[...] = gate
    raw_ref[...] = raw
    step_ref[...] = step_raw
    (col, row, id_col, id_row, _, _, total, step_x, reach_x, leave_x, through_x) = block_setup(
        block, ends_ref, step_raw, head_ref, spread_ref
    )
    ext_ref[0:8, :] = ext_ref[SPAN : SPAN + 8, :]
    ext_ref[8 : SPAN + 8, :] = raw
    pre = taps_ref[4:5, :] + taps_ref[3:4, :] * raw
    for offset in range(1, 4):
        same = jnp.where(ids_at(col + block * SPAN - offset, ends_ref) == id_col, 1.0, 0.0)
        shifted = ext_ref[8 - offset : SPAN + 8 - offset, :]
        pre = pre + taps_ref[3 - offset : 4 - offset, :] * shifted * same
    pre_ref[...] = pre
    conv = (pre * lax.logistic(pre)).astype(jnp.bfloat16)
    conv_ref[...] = conv
    values = conv[:, :inner].astype(jnp.float32)
    in_maps = conv[:, inner : inner + states]
    out_maps = conv[:, inner + states :]
    stepped = (values * step_x).astype(jnp.bfloat16)
    total_rows = total.T
    allowed = (id_col == id_row) & (col >= row)
    inner_prod = contract_last(out_maps, in_maps)
    low_lane = lax.broadcasted_iota(jnp.int32, (1, LANES), 1) < LANES // 2
    state = carry_ref[...]
    state_ref[0] = state
    carried = reach_x * mm(out_maps, state.astype(jnp.bfloat16))
    for pair in range(inner // LANES):
        lanes = slice(pair * LANES, (pair + 1) * LANES)
        parts = []
        for head in (2 * pair, 2 * pair + 1):
            gap = total[:, head : head + 1] - total_rows[head : head + 1, :]
            kernel = jnp.exp(jnp.where(allowed, gap, -1e30))
            parts.append(mm((kernel * inner_prod).astype(jnp.bfloat16), stepped[:, lanes]))
        local = jnp.where(low_lane, parts[0], parts[1])
        ssd = local + carried[:, lanes] + skip_ref[:, lanes] * values[:, lanes]
        ssd_ref[:, lanes] = ssd
        gated_ref[:, lanes] = ssd * (gate[:, lanes] * lax.logistic(gate[:, lanes]))
    leaving = (leave_x * stepped.astype(jnp.float32)).astype(jnp.bfloat16)
    carry_ref[...] = through_x * state + contract_first(in_maps, leaving)


def backward_kernel(
    ends_ref,
    stat_ref,
    normal_ref,
    gate_ref,
    raw_ref,
    pre_ref,
    conv_ref,
    step_ref,
    ssd_ref,
    state_ref,
    next_ref,
    taps_ref,
    head_ref,
    skip_ref,
    gain_ref,
    spread_ref,
    group_ref,
    cols_ref,
    shared_ref,
    taps_grad_ref,
    inner_grad_ref,
    head_grad_ref,
    ext_ref,
    carry_ref,
):
    place = pl.program_id(0)
    block = pl.num_programs(0) - 1 - place
    inner = gate_ref.shape[1]
    width = raw_ref.shape[1]
    states = (width - inner) // 2

    @pl.when(place == 0)
    def _():
        carry_ref[...] = jnp.zeros_like(carry_ref)
        ext_ref[...] = jnp.zeros_like(ext_ref)
        taps_grad_ref[...] = jnp.zeros_like(taps_grad_ref)
        inner_grad_ref[...] = jnp.zeros_like(inner_grad_ref)
        head_grad_ref[...] = jnp.zeros_like(head_grad_ref)

    step_raw = step_ref[...]
    (col, row, id_col, id_row, pre_step, decay, total, step_x, reach_x, leave_x, through_x) = (
        block_setup(block, ends_ref, step_raw, head_ref, spread_ref)
    )
    inv_gate, pull = stat_ref[:, 0:1], stat_ref[:, 1:2]
    d_normal = normal_ref[...]
    gate = gate_ref[...]
    ssd = ssd_ref[...]
    sig = lax.logistic(gate)
    silu = gate * sig
    gated = ssd * silu
    d_gated = inv_gate * (gain_ref[...] * d_normal) - gated * pull
    d_ssd = d_gated * silu
    cols_ref[:, :inner] = (d_gated * ssd * silu_slope(gate, sig)).astype(jnp.bfloat16)
    d_low = d_ssd.astype(jnp.bfloat16)
    d_low_f = d_low.astype(jnp.float32)
    conv = conv_ref[...]
    values = conv[:, :inner].astype(jnp.float32)
    in_maps = conv[:, inner : inner + states]
    out_maps = conv[:, inner + states :]
    inner_grad_ref[0:1, :] += jnp.sum(gated * inv_gate * d_normal, axis=0, keepdims=True)
    inner_grad_ref[1:2, :] += jnp.sum(values * d_ssd, axis=0, keepdims=True)
    stepped = (values * step_x).astype(jnp.bfloat16)
    stepped_f = stepped.astype(jnp.float32)
    total_rows = total.T
    allowed = (id_col == id_row) & (row >= col)
    inner_prod = contract_last(in_maps, out_maps)
    low_lane = lax.broadcasted_iota(jnp.int32, (1, LANES), 1) < LANES // 2
    d_inner = jnp.zeros((SPAN, SPAN), jnp.float32)
    d_stepped = []
    for pair in range(inner // LANES):
        lanes = slice(pair * LANES, (pair + 1) * LANES)
        d_pair = d_low[:, lanes]
        parts = []
        for head in (2 * pair, 2 * pair + 1):
            gap = total_rows[head : head + 1, :] - total[:, head : head + 1]
            kernel = jnp.exp(jnp.where(allowed, gap, -1e30))
            parts.append(mm((kernel * inner_prod).astype(jnp.bfloat16), d_pair))
            own = low_lane if head % 2 == 0 else jnp.logical_not(low_lane)
            own_stepped = jnp.where(own, stepped_f[:, lanes], 0.0).astype(jnp.bfloat16)
            d_inner = d_inner + contract_last(own_stepped, d_pair) * kernel
        d_stepped.append(jnp.where(low_lane, parts[0], parts[1]))
    d_state = carry_ref[...]
    d_state_low = d_state.astype(jnp.bfloat16)
    d_stepped = jnp.concatenate(d_stepped, axis=1) + leave_x * mm(in_maps, d_state_low)
    d_values = step_x * d_stepped + skip_ref[...] * d_ssd
    pulls = d_low_f * (ssd - skip_ref[...] * values) - stepped_f * d_stepped
    ends = jnp.sum(next_ref[0] * d_state, axis=0, keepdims=True)
    grouped = mm(
        split_halves(
            jnp.concatenate(
                [pulls, values * d_stepped, jnp.broadcast_to(ends, (8, inner))], axis=0
            )
        ),
        group_ref[...],
    )
    upper = jnp.where(row >= col, 1.0, 0.0)
    d_decay = (
        jnp.dot(
            upper, grouped[:SPAN], precision=HIGHEST_PREC, preferred_element_type=jnp.float32
        )
        + grouped[2 * SPAN : 2 * SPAN + 1]
    )
    d_step = grouped[SPAN : 2 * SPAN] - jnp.exp(head_ref[0:1, :]) * d_decay
    d_step_raw = d_step * lax.logistic(pre_step)
    head_grad_ref[0:1, :] += jnp.sum(d_decay * decay, axis=0, keepdims=True)
    head_grad_ref[1:2, :] += jnp.sum(d_step_raw, axis=0, keepdims=True)
    reached = (reach_x * d_low_f).astype(jnp.bfloat16)
    leaving = (leave_x * stepped_f).astype(jnp.bfloat16)
    d_inner_low = d_inner.astype(jnp.bfloat16)
    d_out = contract_first(d_inner_low, in_maps) + contract_last(
        reached, state_ref[0].astype(jnp.bfloat16)
    )
    d_in = mm(d_inner_low, out_maps) + contract_last(leaving, d_state_low)
    carry_ref[...] = through_x * d_state + contract_first(out_maps, reached)
    pre = pre_ref[...]
    raw = raw_ref[...]
    d_pre = jnp.concatenate([d_values, d_in, d_out], axis=1) * silu_slope(pre, lax.logistic(pre))
    ext_ref[SPAN : SPAN + 8, :] = ext_ref[0:8, :]
    ext_ref[0:SPAN, :] = d_pre
    d_raw = taps_ref[3:4, :] * d_pre
    taps_grad_ref[3:4, :] += jnp.sum(raw * d_pre, axis=0, keepdims=True)
    taps_grad_ref[4:5, :] += jnp.sum(d_pre, axis=0, keepdims=True)
    for offset in range(1, 4):
        same = jnp.where(ids_at(col + block * SPAN + offset, ends_ref) == id_col, 1.0, 0.0)
        shifted = ext_ref[offset : SPAN + offset, :] * same
        d_raw = d_raw + taps_ref[3 - offset : 4 - offset, :] * shifted
        taps_grad_ref[3 - offset : 4 - offset, :] += jnp.sum(raw * shifted, axis=0, keepdims=True)
    cols_ref[:, inner:] = d_raw[:, :inner].astype(jnp.bfloat16)
    shared_ref[:, : 2 * states] = d_raw[:, inner:]
    shared_ref[:, 2 * states :] = d_step_raw


def whole_spec(array):
    return pl.BlockSpec(array.shape, lambda i: (0,) * array.ndim)


def run_forward(ends, rows, weight, taps, head, skip, spread):
    group_rows = rows.shape[0]
    blocks = group_rows // SPAN
    inner, width = skip.shape[1], taps.shape[1]
    states = (width - inner) // 2

    def rows_spec(columns):
        return pl.BlockSpec((SPAN, columns), lambda i: (i, 0))

    def rows_out(columns, kind):
        return jax.ShapeDtypeStruct((group_rows, columns), kind)

    f32 = jnp.float32
    return pl.pallas_call(
        forward_kernel,
        grid=(blocks,),
        in_specs=[
            pl.BlockSpec(memory_space=pltpu.SMEM),
            rows_spec(rows.shape[1]),
            whole_spec(weight),
            whole_spec(taps),
            whole_spec(head),
            whole_spec(skip),
            whole_spec(spread),
        ],
        out_specs=[
            rows_spec(inner),
            rows_spec(width),
            rows_spec(width),
            rows_spec(width),
            rows_spec(LANES),
            rows_spec(inner),
            rows_spec(inner),
            pl.BlockSpec((1, states, inner), lambda i: (i, 0, 0)),
        ],
        out_shape=[
            rows_out(inner, f32),
            rows_out(width, f32),
            rows_out(width, f32),
            rows_out(width, jnp.bfloat16),
            rows_out(LANES, f32),
            rows_out(inner, f32),
            rows_out(inner, f32),
            jax.ShapeDtypeStruct((blocks, states, inner), f32),
        ],
        scratch_shapes=[
            pltpu.VMEM((SPAN + 8, width), f32),
            pltpu.VMEM((states, inner), f32),
        ],
        compiler_params=pltpu.CompilerParams(
            dimension_semantics=("arbitrary",), vmem_limit_bytes=KERNEL_VMEM
        ),
        cost_estimate=pl.CostEstimate(
            flops=12_000_000_000, bytes_accessed=36_000_000, transcendentals=6_000_000
        ),
        name="scan_forward",
    )(ends, rows, weight, taps, head, skip, spread)


def run_backward(
    ends, stats, d_normal, gate, raw, pre, conv, step, ssd, states_in, taps, head, skip, gain, spread, group
):
    group_rows, inner = gate.shape
    blocks = group_rows // SPAN
    width = raw.shape[1]
    states = states_in.shape[1]

    def rows_spec(columns):
        return pl.BlockSpec((SPAN, columns), lambda i: (blocks - 1 - i, 0))

    def fixed(rows, columns):
        return pl.BlockSpec((rows, columns), lambda i: (0, 0))

    f32 = jnp.float32
    return pl.pallas_call(
        backward_kernel,
        grid=(blocks,),
        in_specs=[
            pl.BlockSpec(memory_space=pltpu.SMEM),
            rows_spec(2),
            rows_spec(inner),
            rows_spec(inner),
            rows_spec(width),
            rows_spec(width),
            rows_spec(width),
            rows_spec(LANES),
            rows_spec(inner),
            pl.BlockSpec((1, states, inner), lambda i: (blocks - 1 - i, 0, 0)),
            pl.BlockSpec((1, states, inner), lambda i: (jnp.minimum(blocks - i, blocks - 1), 0, 0)),
            whole_spec(taps),
            whole_spec(head),
            whole_spec(skip),
            whole_spec(gain),
            whole_spec(spread),
            whole_spec(group),
        ],
        out_specs=[
            rows_spec(2 * inner),
            rows_spec(width - inner + LANES),
            fixed(8, width),
            fixed(8, inner),
            fixed(8, LANES),
        ],
        out_shape=[
            jax.ShapeDtypeStruct((group_rows, 2 * inner), jnp.bfloat16),
            jax.ShapeDtypeStruct((group_rows, width - inner + LANES), f32),
            jax.ShapeDtypeStruct((8, width), f32),
            jax.ShapeDtypeStruct((8, inner), f32),
            jax.ShapeDtypeStruct((8, LANES), f32),
        ],
        scratch_shapes=[
            pltpu.VMEM((SPAN + 8, width), f32),
            pltpu.VMEM((states, inner), f32),
        ],
        compiler_params=pltpu.CompilerParams(
            dimension_semantics=("arbitrary",), vmem_limit_bytes=KERNEL_VMEM
        ),
        cost_estimate=pl.CostEstimate(
            flops=20_000_000_000, bytes_accessed=48_000_000, transcendentals=8_000_000
        ),
        name="scan_backward",
    )(ends, stats, d_normal, gate, raw, pre, conv, step, ssd, states_in, states_in, taps, head, skip, gain, spread, group)


def contract_last(left, right):
    return lax.dot_general(
        left, right, (((1,), (1,)), ((), ())), preferred_element_type=jnp.float32
    )


def contract_first(left, right):
    return lax.dot_general(
        left, right, (((0,), (0,)), ((), ())), preferred_element_type=jnp.float32
    )


def adam_step(weight, grad, first_moment, second_moment, rate, decay_rate):
    first_new = BETA_ONE * first_moment + (1.0 - BETA_ONE) * grad
    second_new = BETA_TWO * second_moment + (1.0 - BETA_TWO) * grad * grad
    first_fix = 1.0 - BETA_ONE**STEP
    second_fix = 1.0 - BETA_TWO**STEP
    update = first_new / first_fix / (jnp.sqrt(second_new / second_fix) + ADAM_EPS)
    return (weight - rate * (update + decay_rate * weight), first_new, second_new)


def swap(vals, axis, bit):
    ways = lax.axis_size(axis)
    return lax.ppermute(vals, axis, [(i, i ^ bit) for i in range(ways)])


def axis_bits(axis):
    return [1 << i for i in range(lax.axis_size(axis).bit_length() - 1)]


def gather_rows(vals, axis, order):
    rows = vals.shape[0]
    ways = lax.axis_size(axis)
    pos = lax.axis_index(axis)
    bits = axis_bits(axis)
    held = vals.reshape((1,) * len(bits) + vals.shape)
    for bit in order:
        dim = len(bits) - bit.bit_length()
        other = swap(held, axis, bit)
        upper = (pos & bit) != 0
        held = jnp.concatenate(
            [jnp.where(upper, other, held), jnp.where(upper, held, other)], axis=dim
        )
    return held.reshape((ways * rows,) + vals.shape[1:])


def scatter_rows(vals, axis, order):
    ways = lax.axis_size(axis)
    pos = lax.axis_index(axis)
    bits = axis_bits(axis)
    rows = vals.shape[0] // ways
    held = vals.reshape((2,) * len(bits) + (rows,) + vals.shape[1:])
    for bit in order:
        dim = len(bits) - bit.bit_length()
        mine = (pos & bit) // bit
        keep = lax.dynamic_slice_in_dim(held, mine, 1, dim)
        send = lax.dynamic_slice_in_dim(held, 1 - mine, 1, dim).astype(jnp.bfloat16)
        held = keep.astype(jnp.float32) + swap(send, axis, bit).astype(jnp.float32)
    return held.reshape((rows,) + vals.shape[1:])


def sum_all(vals, axis):
    for bit in axis_bits(axis):
        vals = vals + swap(vals, axis, bit)
    return vals


def gather_two(vals, axis):
    bits = axis_bits(axis)
    half = (vals.shape[1] // 256) * 128
    return jnp.concatenate(
        [
            gather_rows(vals[:, :half], axis, bits[::-1]),
            gather_rows(vals[:, half:], axis, bits[:1] + bits[:0:-1]),
        ],
        axis=1,
    )


def scatter_two(vals, axis):
    bits = axis_bits(axis)
    half = (vals.shape[1] // 256) * 128
    return jnp.concatenate(
        [
            scatter_rows(vals[:, :half], axis, bits),
            scatter_rows(vals[:, half:], axis, bits[1:] + bits[:1]),
        ],
        axis=1,
    )


def shards(
    tokens,
    cotangent,
    lengths,
    w_heads,
    first_heads,
    second_heads,
    w_shared,
    first_shared,
    second_shared,
    w_out,
    first_out,
    second_out,
    chan_params,
    first_chan,
    second_chan,
    bc_params,
    first_bc,
    second_bc,
    head_params,
    first_head,
    second_head,
    gains,
    first_gains,
    second_gains,
):
    tensor_ways = lax.axis_size("tensor")
    tensor_pos = lax.axis_index("tensor")
    own_rows = tokens.shape[0]
    group_rows = own_rows * tensor_ways
    model_width = tokens.shape[1]
    own_heads = head_params.shape[1]
    all_heads = own_heads * tensor_ways
    own_inner = chan_params.shape[1]
    all_inner = own_inner * tensor_ways
    head_size = own_inner // own_heads
    state_size = bc_params.shape[1] // 2
    seq_ids = segment_ids(lengths[0], group_rows)
    valid_rows = (seq_ids < lengths.shape[1]).astype(jnp.float32)
    own_valid = lax.dynamic_slice_in_dim(valid_rows, tensor_pos * own_rows, own_rows, 0)[:, None]
    norm_gain = gains[:model_width]
    gate_gain = gains[model_width:]
    inputs_f = tokens.astype(jnp.float32)
    norm_scale = lax.rsqrt(jnp.mean(inputs_f * inputs_f, axis=1, keepdims=True) + NORM_EPS)
    normed = (inputs_f * norm_scale * norm_gain[None, :]).astype(jnp.bfloat16)
    gathered = gather_rows(normed, "tensor", (2, 1))
    in_width = w_heads.shape[1]
    heads_low = (
        w_heads.astype(jnp.bfloat16)
        .reshape(-1, own_heads, 2, head_size)
        .transpose(0, 2, 1, 3)
        .reshape(-1, in_width)
    )
    in_full = gather_two(
        jnp.concatenate([heads_low, w_shared.astype(jnp.bfloat16)], axis=1), "dp"
    )
    heads_full, shared_full = in_full[:, :in_width], in_full[:, in_width:]
    out_cols = gather_two(w_out.astype(jnp.bfloat16), "dp")
    step_at = in_width + 2 * state_size
    weight_in = jnp.concatenate(
        [
            in_full[:, :step_at],
            lax.dynamic_slice_in_dim(in_full, step_at + tensor_pos * own_heads, own_heads, 1),
            jnp.zeros((model_width, LANES - own_heads), jnp.bfloat16),
        ],
        axis=1,
    )
    conv_taps = jnp.concatenate([chan_params, bc_params], axis=1)
    head_pad = jnp.pad(head_params, ((0, 0), (0, LANES - own_heads)))
    skip_cols = jnp.repeat(head_params[2], head_size)[None, :]
    spread_one = (
        jnp.arange(own_inner, dtype=jnp.int32)[None, :] // head_size
        == jnp.arange(LANES, dtype=jnp.int32)[:, None]
    ).astype(jnp.bfloat16)
    spread_two = jnp.concatenate([spread_one, spread_one], axis=0)
    group_two = jnp.concatenate([spread_one.T, spread_one.T], axis=0)
    seq_ends = jnp.cumsum(lengths[0])
    gate_cols, raw_cols, pre_cols, conv_cols, step_cols, ssd_cols, gated_vals, states_in = (
        run_forward(seq_ends, gathered, weight_in, conv_taps, head_pad, skip_cols, spread_two)
    )
    cotangent_f = cotangent.astype(jnp.float32)
    masked = (cotangent_f * own_valid).astype(jnp.bfloat16)
    own_gain = lax.dynamic_slice_in_dim(gate_gain, tensor_pos * own_inner, own_inner, 0)[None, :]
    masked_all = gather_rows(masked, "tensor", (2, 1))
    d_normal = jnp.dot(masked_all, out_cols, preferred_element_type=jnp.float32)
    row_sums = lax.psum(
        jnp.stack(
            [
                jnp.sum(gated_vals * gated_vals, axis=1),
                jnp.sum(gated_vals * (d_normal * own_gain), axis=1),
            ]
        ),
        "tensor",
    )
    inv_gate = lax.rsqrt(row_sums[0] / all_inner + NORM_EPS)
    stats = jnp.stack([inv_gate, inv_gate**3 * row_sums[1] / all_inner], axis=1)
    normal_out = (gated_vals * inv_gate[:, None] * own_gain).astype(jnp.bfloat16)
    branch = scatter_rows(contract_last(normal_out, out_cols), "tensor", (1, 2))
    out_grad = contract_first(masked_all, normal_out)
    output = inputs_f + own_valid * branch
    d_cols, d_shared_cols, taps_sums, inner_sums, head_sums = run_backward(
        seq_ends,
        stats,
        d_normal,
        gate_cols,
        raw_cols,
        pre_cols,
        conv_cols,
        step_cols,
        ssd_cols,
        states_in,
        conv_taps,
        head_pad,
        skip_cols,
        own_gain,
        spread_two,
        group_two,
    )
    d_taps = taps_sums[:5]
    gate_gain_grad = lax.dynamic_update_slice_in_dim(
        jnp.zeros((all_inner,), jnp.float32), inner_sums[0], tensor_pos * own_inner, 0
    )
    d_head = jnp.concatenate(
        [
            head_sums[:2, :own_heads],
            jnp.sum(inner_sums[1].reshape(own_heads, head_size), axis=1)[None, :],
        ],
        axis=0,
    )
    d_step_all = lax.dynamic_update_slice_in_dim(
        jnp.zeros((group_rows, all_heads), jnp.float32),
        d_shared_cols[:, 2 * state_size : 2 * state_size + own_heads],
        tensor_pos * own_heads,
        1,
    )
    d_shared_part = jnp.concatenate([d_shared_cols[:, : 2 * state_size], d_step_all], axis=1)
    d_normed_part = contract_last(d_cols, heads_full)
    d_normed_rows, d_shared_rows = (
        scatter_rows(d_normed_part, "tensor", (1, 2)),
        scatter_rows(d_shared_part, "tensor", (1, 2)),
    )
    d_shared_low = d_shared_rows.astype(jnp.bfloat16)
    d_normed = d_normed_rows + contract_last(d_shared_low, shared_full)
    weighted_in = d_normed * norm_gain[None, :]
    in_dot = jnp.sum(inputs_f * weighted_in, axis=1, keepdims=True)
    input_grad = (
        cotangent_f + norm_scale * weighted_in - inputs_f * norm_scale**3 * in_dot / model_width
    )
    heads_grad = contract_first(gathered, d_cols)
    heads_shard, out_shard = (
        scatter_two(heads_grad, "dp"),
        scatter_two(out_grad, "dp"),
    )
    heads_shard = (
        heads_shard.reshape(-1, 2, own_heads, head_size).transpose(0, 2, 1, 3).reshape(-1, in_width)
    )
    norm_gain_grad = jnp.sum(inputs_f * norm_scale * d_normed, axis=0)
    own_sums = sum_all(
        jnp.concatenate(
            [
                norm_gain_grad,
                d_taps[:, own_inner:].reshape(-1),
                gate_gain_grad,
                d_taps[:, :own_inner].reshape(-1),
                d_head.reshape(-1),
            ]
        ),
        "dp",
    )
    shared_part = scatter_rows(
        contract_first(normed, d_shared_low), "dp", axis_bits("dp")
    )
    shared_rows, shared_width = shared_part.shape
    gain_ends = model_width + 10 * state_size
    chan_begin = gain_ends + all_inner
    head_begin = chan_begin + 5 * own_inner
    ring_sums = sum_all(
        jnp.concatenate([own_sums[:chan_begin], shared_part.reshape(-1)]), "tensor"
    )
    gain_sum = jnp.concatenate([ring_sums[:model_width], ring_sums[gain_ends:chan_begin]])
    bc_sum = ring_sums[model_width:gain_ends].reshape(5, 2 * state_size)
    shared_shard = ring_sums[chan_begin:].reshape(shared_rows, shared_width)
    chan_grad = own_sums[chan_begin:head_begin].reshape(5, own_inner)
    head_grad = own_sums[head_begin:].reshape(3, own_heads)
    new_heads, new_first_heads, new_second_heads = adam_step(
        w_heads, heads_shard, first_heads, second_heads, MATRIX_RATE, WEIGHT_DECAY
    )
    new_shared, new_first_shared, new_second_shared = adam_step(
        w_shared, shared_shard, first_shared, second_shared, MATRIX_RATE, WEIGHT_DECAY
    )
    new_out, new_first_out, new_second_out = adam_step(
        w_out, out_shard, first_out, second_out, MATRIX_RATE, WEIGHT_DECAY
    )
    new_chan, new_first_chan, new_second_chan = adam_step(
        chan_params, chan_grad, first_chan, second_chan, SMALL_RATE, 0.0
    )
    new_bc, new_first_bc, new_second_bc = adam_step(
        bc_params, bc_sum, first_bc, second_bc, SMALL_RATE, 0.0
    )
    new_head, new_first_head, new_second_head = adam_step(
        head_params, head_grad, first_head, second_head, HEAD_RATE, 0.0
    )
    new_gains, new_first_gains, new_second_gains = adam_step(
        gains, gain_sum, first_gains, second_gains, GAIN_RATE, 0.0
    )
    return (
        output,
        input_grad,
        new_heads,
        new_first_heads,
        new_second_heads,
        new_shared,
        new_first_shared,
        new_second_shared,
        new_out,
        new_first_out,
        new_second_out,
        new_chan,
        new_first_chan,
        new_second_chan,
        new_bc,
        new_first_bc,
        new_second_bc,
        new_head,
        new_first_head,
        new_second_head,
        new_gains,
        new_first_gains,
        new_second_gains,
    )


def solution(mesh):
    return jax.shard_map(
        shards,
        mesh=mesh,
        in_specs=(
            P(("dp", "tensor"), None),
            P(("dp", "tensor"), None),
            P("dp", None),
            P("dp", "tensor"),
            P("dp", "tensor"),
            P("dp", "tensor"),
            P("dp", None),
            P("dp", None),
            P("dp", None),
            P("dp", "tensor"),
            P("dp", "tensor"),
            P("dp", "tensor"),
            P(None, "tensor"),
            P(None, "tensor"),
            P(None, "tensor"),
            P(),
            P(),
            P(),
            P(None, "tensor"),
            P(None, "tensor"),
            P(None, "tensor"),
            P(),
            P(),
            P(),
        ),
        out_specs=(
            P(("dp", "tensor"), None),
            P(("dp", "tensor"), None),
            P("dp", "tensor"),
            P("dp", "tensor"),
            P("dp", "tensor"),
            P("dp", None),
            P("dp", None),
            P("dp", None),
            P("dp", "tensor"),
            P("dp", "tensor"),
            P("dp", "tensor"),
            P(None, "tensor"),
            P(None, "tensor"),
            P(None, "tensor"),
            P(),
            P(),
            P(),
            P(None, "tensor"),
            P(None, "tensor"),
            P(None, "tensor"),
            P(),
            P(),
            P(),
        ),
        check_vma=False,
    )
```

```python
import jax
import jax.numpy as jnp
from jax import lax
from jax.experimental import pallas as pl
from jax.experimental.pallas import tpu as pltpu
from jax.sharding import PartitionSpec as P

SPAN = 256
STEP = 10


NORM_EPS = 1e-05
BETA_ONE = 0.9
BETA_TWO = 0.95
ADAM_EPS = 1e-08
MATRIX_RATE = 0.03
SMALL_RATE = 0.1
HEAD_RATE = 1.0
GAIN_RATE = 0.5
WEIGHT_DECAY = 0.1
HIGHEST_PREC = lax.Precision.HIGHEST


def segment_ids(seq_lengths, group_rows):
    seq_ends = jnp.cumsum(seq_lengths)
    positions = jnp.arange(group_rows, dtype=jnp.int32)
    return jnp.sum((positions[:, None] >= seq_ends[None, :]).astype(jnp.int32), axis=1)


LANES = 128
KERNEL_VMEM = 56 * 1024 * 1024


def silu_slope(vals, sig):
    return sig * (1.0 + vals * (1.0 - sig))


def split_halves(vals):
    high = vals.astype(jnp.bfloat16)
    rest = (vals - high.astype(jnp.float32)).astype(jnp.bfloat16)
    return jnp.concatenate([high, rest], axis=1)


def mm(left, right):
    return jnp.dot(left, right, preferred_element_type=jnp.float32)


def ids_at(positions, ends_ref):
    ids = jnp.zeros_like(positions)
    for slot in range(ends_ref.shape[0]):
        ids = ids + jnp.where(positions >= ends_ref[slot], 1, 0)
    return ids


def block_setup(block, ends_ref, step_raw, head_ref, spread_ref):
    begin = block * SPAN
    col = lax.broadcasted_iota(jnp.int32, (SPAN, 1), 0)
    row = lax.broadcasted_iota(jnp.int32, (1, SPAN), 1)
    id_col = ids_at(col + begin, ends_ref)
    id_row = ids_at(row + begin, ends_ref)
    prior, last = jnp.int32(0), jnp.int32(0)
    for slot in range(ends_ref.shape[0]):
        prior = prior + jnp.where(begin - 1 >= ends_ref[slot], 1, 0)
        last = last + jnp.where(begin + SPAN - 1 >= ends_ref[slot], 1, 0)
    prior = jnp.where(block == 0, -1, prior)
    pre_step = step_raw + head_ref[1:2, :]
    step = jnp.maximum(pre_step, 0.0) + jnp.log1p(jnp.exp(-jnp.abs(pre_step)))
    decay = -jnp.exp(head_ref[0:1, :]) * step
    lower = jnp.where(col >= row, 1.0, 0.0)
    total = jnp.dot(
        lower, decay, precision=HIGHEST_PREC, preferred_element_type=jnp.float32
    )
    tail = total[SPAN - 1 : SPAN, :]
    reach = jnp.exp(total) * jnp.where(id_col == prior, 1.0, 0.0)
    leave = jnp.exp(tail - total) * jnp.where(id_col == last, 1.0, 0.0)
    through = jnp.exp(tail) * jnp.where(last == prior, 1.0, 0.0)
    stacked = jnp.concatenate([step, reach, leave, jnp.broadcast_to(through, (8, LANES))], axis=0)
    spread = mm(split_halves(stacked), spread_ref[...])
    return (
        col,
        row,
        id_col,
        id_row,
        pre_step,
        decay,
        total,
        spread[:SPAN],
        spread[SPAN : 2 * SPAN],
        spread[2 * SPAN : 3 * SPAN],
        spread[3 * SPAN : 3 * SPAN + 1],
    )


def forward_kernel(
    ends_ref,
    rows_ref,
    weight_ref,
    taps_ref,
    head_ref,
    skip_ref,
    spread_ref,
    gate_ref,
    raw_ref,
    pre_ref,
    conv_ref,
    step_ref,
    ssd_ref,
    gated_ref,
    state_ref,
    ext_ref,
    carry_ref,
):
    block = pl.program_id(0)
    inner = gate_ref.shape[1]
    width = raw_ref.shape[1]
    states = (width - inner) // 2

    @pl.when(block == 0)
    def _():
        carry_ref[...] = jnp.zeros_like(carry_ref)
        ext_ref[...] = jnp.zeros_like(ext_ref)

    cols = mm(rows_ref[...], weight_ref[...])
    gate = cols[:, :inner]
    raw = cols[:, inner : inner + width]
    step_raw = cols[:, inner + width :]
    gate_ref[...] = gate
    raw_ref[...] = raw
    step_ref[...] = step_raw
    (col, row, id_col, id_row, _, _, total, step_x, reach_x, leave_x, through_x) = block_setup(
        block, ends_ref, step_raw, head_ref, spread_ref
    )
    ext_ref[0:8, :] = ext_ref[SPAN : SPAN + 8, :]
    ext_ref[8 : SPAN + 8, :] = raw
    pre = taps_ref[4:5, :] + taps_ref[3:4, :] * raw
    for offset in range(1, 4):
        same = jnp.where(ids_at(col + block * SPAN - offset, ends_ref) == id_col, 1.0, 0.0)
        shifted = ext_ref[8 - offset : SPAN + 8 - offset, :]
        pre = pre + taps_ref[3 - offset : 4 - offset, :] * shifted * same
    pre_ref[...] = pre
    conv = (pre * lax.logistic(pre)).astype(jnp.bfloat16)
    conv_ref[...] = conv
    values = conv[:, :inner].astype(jnp.float32)
    in_maps = conv[:, inner : inner + states]
    out_maps = conv[:, inner + states :]
    stepped = (values * step_x).astype(jnp.bfloat16)
    total_rows = total.T
    allowed = (id_col == id_row) & (col >= row)
    inner_prod = contract_last(out_maps, in_maps)
    low_lane = lax.broadcasted_iota(jnp.int32, (1, LANES), 1) < LANES // 2
    state = carry_ref[...]
    state_ref[0] = state
    carried = reach_x * mm(out_maps, state.astype(jnp.bfloat16))
    for pair in range(inner // LANES):
        lanes = slice(pair * LANES, (pair + 1) * LANES)
        parts = []
        for head in (2 * pair, 2 * pair + 1):
            gap = total[:, head : head + 1] - total_rows[head : head + 1, :]
            kernel = jnp.exp(jnp.where(allowed, gap, -1e30))
            parts.append(mm((kernel * inner_prod).astype(jnp.bfloat16), stepped[:, lanes]))
        local = jnp.where(low_lane, parts[0], parts[1])
        ssd = local + carried[:, lanes] + skip_ref[:, lanes] * values[:, lanes]
        ssd_ref[:, lanes] = ssd
        gated_ref[:, lanes] = ssd * (gate[:, lanes] * lax.logistic(gate[:, lanes]))
    leaving = (leave_x * stepped.astype(jnp.float32)).astype(jnp.bfloat16)
    carry_ref[...] = through_x * state + contract_first(in_maps, leaving)


def backward_kernel(
    ends_ref,
    stat_ref,
    normal_ref,
    gate_ref,
    raw_ref,
    pre_ref,
    conv_ref,
    step_ref,
    ssd_ref,
    state_ref,
    next_ref,
    taps_ref,
    head_ref,
    skip_ref,
    gain_ref,
    spread_ref,
    group_ref,
    cols_ref,
    shared_ref,
    taps_grad_ref,
    inner_grad_ref,
    head_grad_ref,
    ext_ref,
    carry_ref,
):
    place = pl.program_id(0)
    block = pl.num_programs(0) - 1 - place
    inner = gate_ref.shape[1]
    width = raw_ref.shape[1]
    states = (width - inner) // 2

    @pl.when(place == 0)
    def _():
        carry_ref[...] = jnp.zeros_like(carry_ref)
        ext_ref[...] = jnp.zeros_like(ext_ref)
        taps_grad_ref[...] = jnp.zeros_like(taps_grad_ref)
        inner_grad_ref[...] = jnp.zeros_like(inner_grad_ref)
        head_grad_ref[...] = jnp.zeros_like(head_grad_ref)

    step_raw = step_ref[...]
    (col, row, id_col, id_row, pre_step, decay, total, step_x, reach_x, leave_x, through_x) = (
        block_setup(block, ends_ref, step_raw, head_ref, spread_ref)
    )
    inv_gate, pull = stat_ref[:, 0:1], stat_ref[:, 1:2]
    d_normal = normal_ref[...]
    gate = gate_ref[...]
    ssd = ssd_ref[...]
    sig = lax.logistic(gate)
    silu = gate * sig
    gated = ssd * silu
    d_gated = inv_gate * (gain_ref[...] * d_normal) - gated * pull
    d_ssd = d_gated * silu
    cols_ref[:, :inner] = (d_gated * ssd * silu_slope(gate, sig)).astype(jnp.bfloat16)
    d_low = d_ssd.astype(jnp.bfloat16)
    d_low_f = d_low.astype(jnp.float32)
    conv = conv_ref[...]
    values = conv[:, :inner].astype(jnp.float32)
    in_maps = conv[:, inner : inner + states]
    out_maps = conv[:, inner + states :]
    inner_grad_ref[0:1, :] += jnp.sum(gated * inv_gate * d_normal, axis=0, keepdims=True)
    inner_grad_ref[1:2, :] += jnp.sum(values * d_ssd, axis=0, keepdims=True)
    stepped = (values * step_x).astype(jnp.bfloat16)
    stepped_f = stepped.astype(jnp.float32)
    total_rows = total.T
    allowed = (id_col == id_row) & (row >= col)
    inner_prod = contract_last(in_maps, out_maps)
    low_lane = lax.broadcasted_iota(jnp.int32, (1, LANES), 1) < LANES // 2
    d_inner = jnp.zeros((SPAN, SPAN), jnp.float32)
    d_stepped = []
    for pair in range(inner // LANES):
        lanes = slice(pair * LANES, (pair + 1) * LANES)
        d_pair = d_low[:, lanes]
        parts = []
        for head in (2 * pair, 2 * pair + 1):
            gap = total_rows[head : head + 1, :] - total[:, head : head + 1]
            kernel = jnp.exp(jnp.where(allowed, gap, -1e30))
            parts.append(mm((kernel * inner_prod).astype(jnp.bfloat16), d_pair))
            own = low_lane if head % 2 == 0 else jnp.logical_not(low_lane)
            own_stepped = jnp.where(own, stepped_f[:, lanes], 0.0).astype(jnp.bfloat16)
            d_inner = d_inner + contract_last(own_stepped, d_pair) * kernel
        d_stepped.append(jnp.where(low_lane, parts[0], parts[1]))
    d_state = carry_ref[...]
    d_state_low = d_state.astype(jnp.bfloat16)
    d_stepped = jnp.concatenate(d_stepped, axis=1) + leave_x * mm(in_maps, d_state_low)
    d_values = step_x * d_stepped + skip_ref[...] * d_ssd
    pulls = d_low_f * (ssd - skip_ref[...] * values) - stepped_f * d_stepped
    ends = jnp.sum(next_ref[0] * d_state, axis=0, keepdims=True)
    grouped = mm(
        split_halves(
            jnp.concatenate(
                [pulls, values * d_stepped, jnp.broadcast_to(ends, (8, inner))], axis=0
            )
        ),
        group_ref[...],
    )
    upper = jnp.where(row >= col, 1.0, 0.0)
    d_decay = (
        jnp.dot(
            upper, grouped[:SPAN], precision=HIGHEST_PREC, preferred_element_type=jnp.float32
        )
        + grouped[2 * SPAN : 2 * SPAN + 1]
    )
    d_step = grouped[SPAN : 2 * SPAN] - jnp.exp(head_ref[0:1, :]) * d_decay
    d_step_raw = d_step * lax.logistic(pre_step)
    head_grad_ref[0:1, :] += jnp.sum(d_decay * decay, axis=0, keepdims=True)
    head_grad_ref[1:2, :] += jnp.sum(d_step_raw, axis=0, keepdims=True)
    reached = (reach_x * d_low_f).astype(jnp.bfloat16)
    leaving = (leave_x * stepped_f).astype(jnp.bfloat16)
    d_inner_low = d_inner.astype(jnp.bfloat16)
    d_out = contract_first(d_inner_low, in_maps) + contract_last(
        reached, state_ref[0].astype(jnp.bfloat16)
    )
    d_in = mm(d_inner_low, out_maps) + contract_last(leaving, d_state_low)
    carry_ref[...] = through_x * d_state + contract_first(out_maps, reached)
    pre = pre_ref[...]
    raw = raw_ref[...]
    d_pre = jnp.concatenate([d_values, d_in, d_out], axis=1) * silu_slope(pre, lax.logistic(pre))
    ext_ref[SPAN : SPAN + 8, :] = ext_ref[0:8, :]
    ext_ref[0:SPAN, :] = d_pre
    d_raw = taps_ref[3:4, :] * d_pre
    taps_grad_ref[3:4, :] += jnp.sum(raw * d_pre, axis=0, keepdims=True)
    taps_grad_ref[4:5, :] += jnp.sum(d_pre, axis=0, keepdims=True)
    for offset in range(1, 4):
        same = jnp.where(ids_at(col + block * SPAN + offset, ends_ref) == id_col, 1.0, 0.0)
        shifted = ext_ref[offset : SPAN + offset, :] * same
        d_raw = d_raw + taps_ref[3 - offset : 4 - offset, :] * shifted
        taps_grad_ref[3 - offset : 4 - offset, :] += jnp.sum(raw * shifted, axis=0, keepdims=True)
    cols_ref[:, inner:] = d_raw[:, :inner].astype(jnp.bfloat16)
    shared_ref[:, : 2 * states] = d_raw[:, inner:]
    shared_ref[:, 2 * states :] = d_step_raw


def whole_spec(array):
    return pl.BlockSpec(array.shape, lambda i: (0,) * array.ndim)


def run_forward(ends, rows, weight, taps, head, skip, spread):
    group_rows = rows.shape[0]
    blocks = group_rows // SPAN
    inner, width = skip.shape[1], taps.shape[1]
    states = (width - inner) // 2

    def rows_spec(columns):
        return pl.BlockSpec((SPAN, columns), lambda i: (i, 0))

    def rows_out(columns, kind):
        return jax.ShapeDtypeStruct((group_rows, columns), kind)

    f32 = jnp.float32
    return pl.pallas_call(
        forward_kernel,
        grid=(blocks,),
        in_specs=[
            pl.BlockSpec(memory_space=pltpu.SMEM),
            rows_spec(rows.shape[1]),
            whole_spec(weight),
            whole_spec(taps),
            whole_spec(head),
            whole_spec(skip),
            whole_spec(spread),
        ],
        out_specs=[
            rows_spec(inner),
            rows_spec(width),
            rows_spec(width),
            rows_spec(width),
            rows_spec(LANES),
            rows_spec(inner),
            rows_spec(inner),
            pl.BlockSpec((1, states, inner), lambda i: (i, 0, 0)),
        ],
        out_shape=[
            rows_out(inner, f32),
            rows_out(width, f32),
            rows_out(width, f32),
            rows_out(width, jnp.bfloat16),
            rows_out(LANES, f32),
            rows_out(inner, f32),
            rows_out(inner, f32),
            jax.ShapeDtypeStruct((blocks, states, inner), f32),
        ],
        scratch_shapes=[
            pltpu.VMEM((SPAN + 8, width), f32),
            pltpu.VMEM((states, inner), f32),
        ],
        compiler_params=pltpu.CompilerParams(
            dimension_semantics=("arbitrary",), vmem_limit_bytes=KERNEL_VMEM
        ),
        cost_estimate=pl.CostEstimate(
            flops=12_000_000_000, bytes_accessed=36_000_000, transcendentals=6_000_000
        ),
        name="scan_forward",
    )(ends, rows, weight, taps, head, skip, spread)


def run_backward(
    ends, stats, d_normal, gate, raw, pre, conv, step, ssd, states_in, taps, head, skip, gain, spread, group
):
    group_rows, inner = gate.shape
    blocks = group_rows // SPAN
    width = raw.shape[1]
    states = states_in.shape[1]

    def rows_spec(columns):
        return pl.BlockSpec((SPAN, columns), lambda i: (blocks - 1 - i, 0))

    def fixed(rows, columns):
        return pl.BlockSpec((rows, columns), lambda i: (0, 0))

    f32 = jnp.float32
    return pl.pallas_call(
        backward_kernel,
        grid=(blocks,),
        in_specs=[
            pl.BlockSpec(memory_space=pltpu.SMEM),
            rows_spec(2),
            rows_spec(inner),
            rows_spec(inner),
            rows_spec(width),
            rows_spec(width),
            rows_spec(width),
            rows_spec(LANES),
            rows_spec(inner),
            pl.BlockSpec((1, states, inner), lambda i: (blocks - 1 - i, 0, 0)),
            pl.BlockSpec((1, states, inner), lambda i: (jnp.minimum(blocks - i, blocks - 1), 0, 0)),
            whole_spec(taps),
            whole_spec(head),
            whole_spec(skip),
            whole_spec(gain),
            whole_spec(spread),
            whole_spec(group),
        ],
        out_specs=[
            rows_spec(2 * inner),
            rows_spec(width - inner + LANES),
            fixed(8, width),
            fixed(8, inner),
            fixed(8, LANES),
        ],
        out_shape=[
            jax.ShapeDtypeStruct((group_rows, 2 * inner), jnp.bfloat16),
            jax.ShapeDtypeStruct((group_rows, width - inner + LANES), f32),
            jax.ShapeDtypeStruct((8, width), f32),
            jax.ShapeDtypeStruct((8, inner), f32),
            jax.ShapeDtypeStruct((8, LANES), f32),
        ],
        scratch_shapes=[
            pltpu.VMEM((SPAN + 8, width), f32),
            pltpu.VMEM((states, inner), f32),
        ],
        compiler_params=pltpu.CompilerParams(
            dimension_semantics=("arbitrary",), vmem_limit_bytes=KERNEL_VMEM
        ),
        cost_estimate=pl.CostEstimate(
            flops=20_000_000_000, bytes_accessed=48_000_000, transcendentals=8_000_000
        ),
        name="scan_backward",
    )(ends, stats, d_normal, gate, raw, pre, conv, step, ssd, states_in, states_in, taps, head, skip, gain, spread, group)


def contract_last(left, right):
    return lax.dot_general(
        left, right, (((1,), (1,)), ((), ())), preferred_element_type=jnp.float32
    )


def contract_first(left, right):
    return lax.dot_general(
        left, right, (((0,), (0,)), ((), ())), preferred_element_type=jnp.float32
    )


def adam_step(weight, grad, first_moment, second_moment, rate, decay_rate):
    first_new = BETA_ONE * first_moment + (1.0 - BETA_ONE) * grad
    second_new = BETA_TWO * second_moment + (1.0 - BETA_TWO) * grad * grad
    first_fix = 1.0 - BETA_ONE**STEP
    second_fix = 1.0 - BETA_TWO**STEP
    update = first_new / first_fix / (jnp.sqrt(second_new / second_fix) + ADAM_EPS)
    return (weight - rate * (update + decay_rate * weight), first_new, second_new)


def swap(vals, axis, bit):
    ways = lax.axis_size(axis)
    return lax.ppermute(vals, axis, [(i, i ^ bit) for i in range(ways)])


def axis_bits(axis):
    return [1 << i for i in range(lax.axis_size(axis).bit_length() - 1)]


def gather_rows(vals, axis, order):
    rows = vals.shape[0]
    ways = lax.axis_size(axis)
    pos = lax.axis_index(axis)
    bits = axis_bits(axis)
    held = vals.reshape((1,) * len(bits) + vals.shape)
    for bit in order:
        dim = len(bits) - bit.bit_length()
        other = swap(held, axis, bit)
        upper = (pos & bit) != 0
        held = jnp.concatenate(
            [jnp.where(upper, other, held), jnp.where(upper, held, other)], axis=dim
        )
    return held.reshape((ways * rows,) + vals.shape[1:])


def halve_rows(held, axis, order):
    pos = lax.axis_index(axis)
    for bit in order:
        half = held.shape[0] // 2
        mine = (pos & bit) // bit
        keep = lax.dynamic_slice_in_dim(held, mine * half, half, 0)
        send = lax.dynamic_slice_in_dim(held, (1 - mine) * half, half, 0).astype(jnp.bfloat16)
        held = keep.astype(jnp.float32) + swap(send, axis, bit).astype(jnp.float32)
    return held[0]


def scatter_rows(vals, axis, order):
    ways = lax.axis_size(axis)
    depth = len(axis_bits(axis))
    rows, columns = vals.shape[0] // ways, vals.shape[1]
    held = vals.astype(jnp.bfloat16).reshape((2,) * depth + (rows, columns))
    dims = [depth - bit.bit_length() for bit in order] + [depth, depth + 1]
    return halve_rows(held.transpose(dims).reshape(ways, rows, columns), axis, order)


def scatter_product(left, right, axis):
    ways = lax.axis_size(axis)
    core = lax.axis_index(axis) & 1
    rows = left.shape[0] // ways
    blocks = left.reshape(ways // 2, 2, rows, left.shape[1])
    send_rows = lax.dynamic_slice_in_dim(blocks, 1 - core, 1, 1).reshape(-1, left.shape[1])
    keep_rows = lax.dynamic_slice_in_dim(blocks, core, 1, 1).reshape(-1, left.shape[1])
    got = swap(contract_last(send_rows, right).astype(jnp.bfloat16), axis, 1)
    held = contract_last(keep_rows, right) + got.astype(jnp.float32)
    return halve_rows(
        held.reshape(ways // 2, rows, right.shape[0]), axis, axis_bits(axis)[:0:-1]
    )


def sum_all(vals, axis):
    bits = axis_bits(axis)
    while bits:
        group, bits = bits[:3], bits[3:]
        parts = [vals] + [swap(vals, axis, group[0] * i) for i in range(1, 1 << len(group))]
        while len(parts) > 1:
            parts = [parts[i] + parts[i + 1] for i in range(0, len(parts), 2)]
        vals = parts[0]
    return vals


def gather_two(vals, axis):
    bits = axis_bits(axis)
    half = (vals.shape[1] // 256) * 128
    return jnp.concatenate(
        [
            gather_rows(vals[:, :half], axis, bits[::-1]),
            gather_rows(vals[:, half:], axis, bits[:1] + bits[:0:-1]),
        ],
        axis=1,
    )


def scatter_two(vals, axis):
    bits = axis_bits(axis)
    half = (vals.shape[1] // 256) * 128
    return jnp.concatenate(
        [
            scatter_rows(vals[:, :half], axis, bits),
            scatter_rows(vals[:, half:], axis, bits[1:] + bits[:1]),
        ],
        axis=1,
    )


def shards(
    tokens,
    cotangent,
    lengths,
    w_heads,
    first_heads,
    second_heads,
    w_shared,
    first_shared,
    second_shared,
    w_out,
    first_out,
    second_out,
    chan_params,
    first_chan,
    second_chan,
    bc_params,
    first_bc,
    second_bc,
    head_params,
    first_head,
    second_head,
    gains,
    first_gains,
    second_gains,
):
    tensor_ways = lax.axis_size("tensor")
    tensor_pos = lax.axis_index("tensor")
    own_rows = tokens.shape[0]
    group_rows = own_rows * tensor_ways
    model_width = tokens.shape[1]
    own_heads = head_params.shape[1]
    all_heads = own_heads * tensor_ways
    own_inner = chan_params.shape[1]
    all_inner = own_inner * tensor_ways
    head_size = own_inner // own_heads
    state_size = bc_params.shape[1] // 2
    seq_ids = segment_ids(lengths[0], group_rows)
    valid_rows = (seq_ids < lengths.shape[1]).astype(jnp.float32)
    own_valid = lax.dynamic_slice_in_dim(valid_rows, tensor_pos * own_rows, own_rows, 0)[:, None]
    norm_gain = gains[:model_width]
    gate_gain = gains[model_width:]
    inputs_f = tokens.astype(jnp.float32)
    norm_scale = lax.rsqrt(jnp.mean(inputs_f * inputs_f, axis=1, keepdims=True) + NORM_EPS)
    normed = (inputs_f * norm_scale * norm_gain[None, :]).astype(jnp.bfloat16)
    gathered = gather_rows(normed, "tensor", (2, 1))
    in_width = w_heads.shape[1]
    heads_low = (
        w_heads.astype(jnp.bfloat16)
        .reshape(-1, own_heads, 2, head_size)
        .transpose(0, 2, 1, 3)
        .reshape(-1, in_width)
    )
    in_full = gather_two(
        jnp.concatenate([heads_low, w_shared.astype(jnp.bfloat16)], axis=1), "dp"
    )
    heads_full, shared_full = in_full[:, :in_width], in_full[:, in_width:]
    out_cols = gather_two(w_out.astype(jnp.bfloat16), "dp")
    step_at = in_width + 2 * state_size
    weight_in = jnp.concatenate(
        [
            in_full[:, :step_at],
            lax.dynamic_slice_in_dim(in_full, step_at + tensor_pos * own_heads, own_heads, 1),
            jnp.zeros((model_width, LANES - own_heads), jnp.bfloat16),
        ],
        axis=1,
    )
    conv_taps = jnp.concatenate([chan_params, bc_params], axis=1)
    head_pad = jnp.pad(head_params, ((0, 0), (0, LANES - own_heads)))
    skip_cols = jnp.repeat(head_params[2], head_size)[None, :]
    spread_one = (
        jnp.arange(own_inner, dtype=jnp.int32)[None, :] // head_size
        == jnp.arange(LANES, dtype=jnp.int32)[:, None]
    ).astype(jnp.bfloat16)
    spread_two = jnp.concatenate([spread_one, spread_one], axis=0)
    group_two = jnp.concatenate([spread_one.T, spread_one.T], axis=0)
    seq_ends = jnp.cumsum(lengths[0])
    gate_cols, raw_cols, pre_cols, conv_cols, step_cols, ssd_cols, gated_vals, states_in = (
        run_forward(seq_ends, gathered, weight_in, conv_taps, head_pad, skip_cols, spread_two)
    )
    cotangent_f = cotangent.astype(jnp.float32)
    masked = (cotangent_f * own_valid).astype(jnp.bfloat16)
    own_gain = lax.dynamic_slice_in_dim(gate_gain, tensor_pos * own_inner, own_inner, 0)[None, :]
    masked_all = gather_rows(masked, "tensor", (2, 1))
    d_normal = jnp.dot(masked_all, out_cols, preferred_element_type=jnp.float32)
    row_sums = lax.psum(
        jnp.stack(
            [
                jnp.sum(gated_vals * gated_vals, axis=1),
                jnp.sum(gated_vals * (d_normal * own_gain), axis=1),
            ]
        ),
        "tensor",
    )
    inv_gate = lax.rsqrt(row_sums[0] / all_inner + NORM_EPS)
    stats = jnp.stack([inv_gate, inv_gate**3 * row_sums[1] / all_inner], axis=1)
    normal_out = (gated_vals * inv_gate[:, None] * own_gain).astype(jnp.bfloat16)
    branch = scatter_product(normal_out, out_cols, "tensor")
    out_grad = contract_first(masked_all, normal_out)
    output = inputs_f + own_valid * branch
    d_cols, d_shared_cols, taps_sums, inner_sums, head_sums = run_backward(
        seq_ends,
        stats,
        d_normal,
        gate_cols,
        raw_cols,
        pre_cols,
        conv_cols,
        step_cols,
        ssd_cols,
        states_in,
        conv_taps,
        head_pad,
        skip_cols,
        own_gain,
        spread_two,
        group_two,
    )
    d_taps = taps_sums[:5]
    gate_gain_grad = lax.dynamic_update_slice_in_dim(
        jnp.zeros((all_inner,), jnp.float32), inner_sums[0], tensor_pos * own_inner, 0
    )
    d_head = jnp.concatenate(
        [
            head_sums[:2, :own_heads],
            jnp.sum(inner_sums[1].reshape(own_heads, head_size), axis=1)[None, :],
        ],
        axis=0,
    )
    d_step_all = lax.dynamic_update_slice_in_dim(
        jnp.zeros((group_rows, all_heads), jnp.float32),
        d_shared_cols[:, 2 * state_size : 2 * state_size + own_heads],
        tensor_pos * own_heads,
        1,
    )
    d_shared_part = jnp.concatenate([d_shared_cols[:, : 2 * state_size], d_step_all], axis=1)
    d_normed_rows, d_shared_rows = (
        scatter_product(d_cols, heads_full, "tensor"),
        scatter_rows(d_shared_part, "tensor", (1, 2)),
    )
    d_shared_low = d_shared_rows.astype(jnp.bfloat16)
    d_normed = d_normed_rows + contract_last(d_shared_low, shared_full)
    weighted_in = d_normed * norm_gain[None, :]
    in_dot = jnp.sum(inputs_f * weighted_in, axis=1, keepdims=True)
    input_grad = (
        cotangent_f + norm_scale * weighted_in - inputs_f * norm_scale**3 * in_dot / model_width
    )
    dp_bits = axis_bits("dp")
    gate_shard = scatter_rows(contract_first(gathered, d_cols[:, :own_inner]), "dp", dp_bits)
    value_shard = scatter_rows(
        contract_first(gathered, d_cols[:, own_inner:]), "dp", dp_bits[1:] + dp_bits[:1]
    )
    out_shard = scatter_two(out_grad, "dp")
    heads_shard = (
        jnp.concatenate([gate_shard, value_shard], axis=1).reshape(-1, 2, own_heads, head_size).transpose(0, 2, 1, 3).reshape(-1, in_width)
    )
    norm_gain_grad = jnp.sum(inputs_f * norm_scale * d_normed, axis=0)
    own_sums = sum_all(
        jnp.concatenate(
            [
                d_taps[:, own_inner:].reshape(-1),
                gate_gain_grad,
                d_taps[:, :own_inner].reshape(-1),
                d_head.reshape(-1),
            ]
        ),
        "dp",
    )
    shared_part = scatter_rows(
        contract_first(normed, d_shared_low), "dp", axis_bits("dp")
    )
    bc_ends = 10 * state_size
    chan_begin = bc_ends + all_inner
    head_begin = chan_begin + 5 * own_inner
    ring_sums = sum_all(own_sums[:chan_begin], "tensor")
    shared_shard = sum_all(shared_part, "tensor")
    gain_sum = jnp.concatenate(
        [sum_all(sum_all(norm_gain_grad, "dp"), "tensor"), ring_sums[bc_ends:]]
    )
    bc_sum = ring_sums[:bc_ends].reshape(5, 2 * state_size)
    chan_grad = own_sums[chan_begin:head_begin].reshape(5, own_inner)
    head_grad = own_sums[head_begin:].reshape(3, own_heads)
    new_heads, new_first_heads, new_second_heads = adam_step(
        w_heads, heads_shard, first_heads, second_heads, MATRIX_RATE, WEIGHT_DECAY
    )
    new_shared, new_first_shared, new_second_shared = adam_step(
        w_shared, shared_shard, first_shared, second_shared, MATRIX_RATE, WEIGHT_DECAY
    )
    new_out, new_first_out, new_second_out = adam_step(
        w_out, out_shard, first_out, second_out, MATRIX_RATE, WEIGHT_DECAY
    )
    new_chan, new_first_chan, new_second_chan = adam_step(
        chan_params, chan_grad, first_chan, second_chan, SMALL_RATE, 0.0
    )
    new_bc, new_first_bc, new_second_bc = adam_step(
        bc_params, bc_sum, first_bc, second_bc, SMALL_RATE, 0.0
    )
    new_head, new_first_head, new_second_head = adam_step(
        head_params, head_grad, first_head, second_head, HEAD_RATE, 0.0
    )
    new_gains, new_first_gains, new_second_gains = adam_step(
        gains, gain_sum, first_gains, second_gains, GAIN_RATE, 0.0
    )
    return (
        output,
        input_grad,
        new_heads,
        new_first_heads,
        new_second_heads,
        new_shared,
        new_first_shared,
        new_second_shared,
        new_out,
        new_first_out,
        new_second_out,
        new_chan,
        new_first_chan,
        new_second_chan,
        new_bc,
        new_first_bc,
        new_second_bc,
        new_head,
        new_first_head,
        new_second_head,
        new_gains,
        new_first_gains,
        new_second_gains,
    )


def solution(mesh):
    return jax.shard_map(
        shards,
        mesh=mesh,
        in_specs=(
            P(("dp", "tensor"), None),
            P(("dp", "tensor"), None),
            P("dp", None),
            P("dp", "tensor"),
            P("dp", "tensor"),
            P("dp", "tensor"),
            P("dp", None),
            P("dp", None),
            P("dp", None),
            P("dp", "tensor"),
            P("dp", "tensor"),
            P("dp", "tensor"),
            P(None, "tensor"),
            P(None, "tensor"),
            P(None, "tensor"),
            P(),
            P(),
            P(),
            P(None, "tensor"),
            P(None, "tensor"),
            P(None, "tensor"),
            P(),
            P(),
            P(),
        ),
        out_specs=(
            P(("dp", "tensor"), None),
            P(("dp", "tensor"), None),
            P("dp", "tensor"),
            P("dp", "tensor"),
            P("dp", "tensor"),
            P("dp", None),
            P("dp", None),
            P("dp", None),
            P("dp", "tensor"),
            P("dp", "tensor"),
            P("dp", "tensor"),
            P(None, "tensor"),
            P(None, "tensor"),
            P(None, "tensor"),
            P(),
            P(),
            P(),
            P(None, "tensor"),
            P(None, "tensor"),
            P(None, "tensor"),
            P(),
            P(),
            P(),
        ),
        check_vma=False,
    )
```
